128 devices in a mesh: dp: 8 (over z, x_lo), owner: 16 (over x_hi, y, core).
Axes of the slice: x: 4 (x_hi: 2, x_lo: 2; x = x_hi * 2 + x_lo), y: 4, z: 4, core: 2. Of those that a mesh axis runs over, the one named last changes fastest.
Arguments:
- activations: bfloat16 [131072, 8192], P(('dp', 'owner')), may hold values from -12 to 12
- gradient: bfloat16 [8192, 4096], P(None, ('dp', 'owner')), may hold values from -6 to 6
- iterations: int32 [32], replicated, may hold values from 5 to 8
Outputs:
- preconditioned: bfloat16 [8192, 4096], P(None, 'dp')
The draws below stay inside these ranges and needn't reach their ends.
All inputs are finite; a program needn't handle non-finite values. Where the reference program divides by a largest or mean magnitude, that divisor is 1e-20 or more.
Results may differ from the reference program's by a relative error of at most 0.012.
Values may be sent and summed in bfloat16 or wider, within the bound.
A program may use at most 192 MiB of HBM per device.

```python
import math
import jax
import jax.numpy as jnp
from jax import lax

D = 8192
F = 4096
BS = 256
ITERS = 8
NB = 32
TOKENS = 131072


def draw_activations(key, part):
    key = jax.random.fold_in(key, 7)
    scale_key, value_key, latent_key, loading_key = jax.random.split(key, 4)
    scales = jnp.exp(jax.random.uniform(scale_key, (D,), jnp.float32, math.log(0.3), math.log(3.0)))
    values = jax.random.truncated_normal(value_key, -4.0, 4.0, (TOKENS, D), jnp.float32)
    latent = jax.random.truncated_normal(latent_key, -4.0, 4.0, (TOKENS, 32), jnp.float32)
    strength = 1.0
    loadings = jax.random.normal(loading_key, (32, D), jnp.float32) * (strength / math.sqrt(32.0))
    mixed = values + jnp.dot(latent, loadings, precision=lax.Precision.HIGHEST)
    return (4.0 * jnp.tanh(mixed / 4.0) * scales[None, :]).astype(jnp.bfloat16)


def with_ends(values, rng, low, top_value):
    index_at = [jax.random.randint(jax.random.fold_in(rng, axis), (), 0, length) for axis, length in enumerate(values.shape)]
    main_axis = values.shape.index(max(values.shape))
    next_to = index_at[:main_axis] + [(index_at[main_axis] + 1) % values.shape[main_axis]] + index_at[main_axis + 1:]
    return values.at[tuple(index_at)].set(low).at[tuple(next_to)].set(top_value)


def steps_of(stream_key, extent, cuts, least, high):
    factor_of = 1.0
    for axis_at, blocks in cuts:
        steps = jax.random.uniform(jax.random.fold_in(jax.random.fold_in(stream_key, 6), axis_at), (blocks,), jnp.float32, least / len(cuts), high / len(cuts))
        factor_of = factor_of * jnp.repeat(jnp.exp(steps), extent[axis_at] // blocks).reshape((-1,) + (1,) * (len(extent) - 1 - axis_at))
    return factor_of


def scatter_about(own_key, dims, deviation, limit, shards=(), held_as=jnp.bfloat16):
    array = deviation * jax.random.normal(own_key, dims, jnp.float32)
    if shards:
        array = array * steps_of(own_key, dims, shards, -0.22, 0.18)
    return jnp.clip(array, -limit, limit).astype(held_as)


def setup_inputs(seed: int = 0) -> dict:
    splits = jax.random.split(jax.random.key(seed), 4)
    activations = draw_activations(jax.random.fold_in(splits[3], 71), 0)
    gradient = scatter_about(splits[1], (D, F), 1.0, 6.0, ((1, 128),))
    iterations = with_ends(jax.random.randint(splits[2], (NB,), ITERS - 3, ITERS + 1), jax.random.fold_in(splits[2], 1), ITERS - 3, ITERS).astype(jnp.int32)
    return dict(activations=activations, gradient=gradient, iterations=iterations)


damping = 0.1


def reference(activations, gradient, iterations):
    identity = jnp.eye(BS, dtype=jnp.float32)

    def one_block(block):
        columns = lax.dynamic_slice_in_dim(activations, block * BS, BS, 1)
        grad_rows = lax.dynamic_slice_in_dim(gradient, block * BS, BS, 0)
        covariance = jnp.dot(columns.T, columns, preferred_element_type=jnp.float32) / TOKENS
        damped = covariance + damping * identity
        row_bound = jnp.max(jnp.sum(jnp.abs(damped), axis=1))
        start = identity / row_bound

        def newton(step_index, approx):
            product = jnp.dot(damped, approx, precision=lax.Precision.HIGHEST)
            return 2.0 * approx - jnp.dot(approx, product, precision=lax.Precision.HIGHEST)

        approx = lax.fori_loop(0, iterations[block], newton, start)
        inverse = approx.astype(jnp.bfloat16)
        return jnp.dot(inverse, grad_rows, preferred_element_type=jnp.float32).astype(jnp.bfloat16)

    result = lax.map(one_block, jnp.arange(NB, dtype=jnp.int32))
    return result.reshape(D, F)
```

```python
import functools

import jax
import jax.numpy as jnp
from jax import lax
from jax.experimental import pallas as pl
from jax.experimental.pallas import tpu as pltpu
from jax.sharding import PartitionSpec as P

BS = 256
HALF = BS // 2
BLOCKS = 32
PACK = BS + 16
TOKENS = 131072
DAMPING = 0.1
ITERS = 8
LEAST_ITERS = 5
SIDE = 4
GROUP = 4
GROUP_COLS = GROUP * BS
CLASS = 16
MESH = pl.DeviceIdType.MESH

TN = (((0,), (0,)), ((), ()))
NT = (((1,), (1,)), ((), ()))


def here():
    shard = lax.axis_index("dp")
    owner = lax.axis_index("owner")
    x = (owner // 8) * 2 + shard % 2
    return x, (owner // 2) % 4, shard // 2, owner % 2


def mesh_id(x, y, z, core):
    return (z * 2 + x % 2, (x // 2) * 8 + y * 2 + core)


def owner_of(x, y, core):
    return (x // 2) * 8 + y * 2 + core


def tile_iota():
    rows = lax.broadcasted_iota(jnp.int32, (HALF, HALF), 0)
    cols = lax.broadcasted_iota(jnp.int32, (HALF, HALF), 1)
    return rows, cols


def pack(block):
    rows, cols = tile_iota()
    low = block[HALF:, HALF:]
    mixed = jnp.where(rows <= cols, block[:HALF, :HALF], low)
    diagonal = jnp.sum(jnp.where(rows == cols, low, 0.0), axis=0, keepdims=True)
    return mixed, block[:HALF, HALF:], jnp.broadcast_to(diagonal, (16, HALF))


def unpack(mixed, off, diagonal):
    rows, cols = tile_iota()
    turned = mixed.T
    first = jnp.where(rows <= cols, mixed, turned)
    second = jnp.where(rows > cols, mixed, jnp.where(rows < cols, turned, diagonal))
    return first, off, off.T, second


def split(value):
    high = value.astype(jnp.bfloat16)
    return high, (value - high.astype(jnp.float32)).astype(jnp.bfloat16)


def dot3(left, right):
    lh, ll = split(left)
    rh, rl = split(right)
    mul = functools.partial(jnp.dot, preferred_element_type=jnp.float32)
    return mul(lh, rh) + (mul(lh, rl) + mul(ll, rh))


def newton(factor, count):
    rows = lax.broadcasted_iota(jnp.int32, (BS, BS), 0)
    cols = lax.broadcasted_iota(jnp.int32, (BS, BS), 1)
    identity = jnp.where(rows == cols, 1.0, 0.0)
    damped = factor / TOKENS + DAMPING * identity
    bound = jnp.max(jnp.sum(jnp.abs(damped), axis=1))
    ratio = damped / bound
    approx = (2.0 * identity - ratio) / bound
    ratio = 2.0 * ratio - dot3(ratio, ratio)
    for step in range(1, ITERS):
        if step < ITERS - 1:
            both = dot3(jnp.concatenate([ratio, approx], axis=0), ratio)
            later = 2.0 * approx - both[BS:]
            ratio = 2.0 * ratio - both[:BS]
        else:
            later = 2.0 * approx - dot3(approx, ratio)
        approx = later if step < LEAST_ITERS else jnp.where(step < count, later, approx)
    return approx


def factor_kernel(
    act_ref, grad_ref, iters_ref,
    full_ref, inv_ref,
    act, to_sib, from_sib, own, summed, landed, y_terms, inv_own,
    act_sem, sib_send, sib_recv, rs_send, rs_recv, y_send, y_recv,
    ag_send, ag_recv, ags_send, ags_recv,
    g_local, g_send, g_recv, gs_send, gs_recv,
):
    x, y, z, core = here()
    sibling = mesh_id(x, y, z, 1 - core)

    def at(dx, dy, dz):
        return mesh_id((x + dx) % SIDE, (y + dy) % SIDE, (z + dz) % SIDE, core)

    plane = [(dz, dx) for dz in (1, 2, 3, 0) for dx in range(SIDE) if dz or dx]

    def remote(src, dst, send, recv, target):
        return pltpu.make_async_remote_copy(
            src_ref=src, dst_ref=dst, send_sem=send, recv_sem=recv, device_id=target, device_id_type=MESH
        )

    def act_copy(slot):
        side = jnp.where(slot < 4, 1 - core, core)
        group = side * 4 + (z + slot % 4 + 1) % SIDE
        cols = pl.ds(pl.multiple_of(group * GROUP_COLS, GROUP_COLS), GROUP_COLS)
        return pltpu.make_async_copy(act_ref.at[:, cols], act.at[slot], act_sem.at[slot])

    for slot in range(8):
        act_copy(slot).start()

    barrier = pltpu.get_barrier_semaphore()
    partners = [sibling] + [at(dx, 0, dz) for dz, dx in plane] + [at(0, dy, 0) for dy in (1, 2, 3)]
    for partner in partners:
        pl.semaphore_signal(barrier, inc=1, device_id=partner, device_id_type=MESH)
    pl.semaphore_wait(barrier, len(partners))

    def rows_of(dx, dy, side):
        first = owner_of((x + dx) % SIDE, (y + dy) % SIDE, side) * 32
        return pl.ds(pl.multiple_of(first, 32), 32)

    def shard(dx, dy, side=core):
        return full_ref.at[rows_of(dx, dy, side)]

    mine = pltpu.make_async_copy(grad_ref, shard(0, 0), g_local)
    mine.start()
    g_copies = []
    first_copy = remote(grad_ref, shard(0, 0), g_send.at[0], g_recv.at[0], at(2, 0, 0))
    first_copy.start()
    for dy in (1, 3, 2):
        copy = remote(grad_ref, shard(0, 0), g_send.at[dy], g_recv.at[dy], at(0, dy, 0))
        copy.start()
        g_copies.append(copy)
    own_to_sib = remote(grad_ref, shard(0, 0), gs_send.at[0], gs_recv.at[0], sibling)
    own_to_sib.start()

    def products(slot, store):
        act_copy(slot).wait()
        for j in range(GROUP):
            cols = act[slot, :, j * BS : (j + 1) * BS]
            mixed, off, diagonal = pack(lax.dot_general(cols, cols, TN, preferred_element_type=jnp.float32))
            store(j, 0, HALF, mixed)
            store(j, HALF, HALF, off)
            store(j, BS, 16, diagonal)

    def sib_copy(k):
        return remote(to_sib.at[k], from_sib.at[k], sib_send.at[k], sib_recv.at[k], sibling)

    def sibling_group(k, carry):
        def store(j, first, rows, value):
            to_sib[k, j, pl.ds(first, rows), :] = value.astype(jnp.bfloat16)

        products(k, store)
        sib_copy(k).start()
        return carry

    lax.fori_loop(0, 4, sibling_group, 0)

    def rs_copy(dz, dx):
        k = (dz + 3) % 4
        slot = dz * 4 + dx
        return remote(
            summed.at[k, (x + dx) % SIDE], landed.at[slot], rs_send.at[slot], rs_recv.at[slot], at(dx, 0, dz)
        )

    def own_products(k):
        def store(j, first, rows, value):
            own[j, pl.ds(first, rows), :] = value

        products(4 + k, store)
        sib_copy(k).wait_recv()
        summed[k] = (own[...] + from_sib[k].astype(jnp.float32)).astype(jnp.bfloat16)

    for k in range(4):
        own_products(k)
        for dx in range(SIDE):
            if k < 3 or dx:
                rs_copy((k + 1) % 4, dx).start()

    first_copy.wait_recv()
    second_copies = []
    for dy in (1, 3, 2):
        copy = remote(shard(2, 0), shard(2, 0), g_send.at[3 + dy], g_recv.at[3 + dy], at(0, dy, 0))
        copy.start()
        second_copies.append(copy)
    partner_to_sib = remote(shard(2, 0), shard(2, 0), gs_send.at[1], gs_recv.at[1], sibling)
    partner_to_sib.start()

    total = summed[3, pl.ds(x, 1)][0].astype(jnp.float32)
    for dz, dx in plane:
        rs_copy(dz, dx).wait_recv()
        total = total + landed[dz * 4 + dx].astype(jnp.float32)
    y_terms[pl.ds(y, 1)] = total.astype(jnp.bfloat16)[None]

    def y_copy(dy):
        return remote(y_terms.at[y], y_terms.at[y], y_send.at[dy], y_recv.at[dy], at(0, dy, 0))

    for dy in (1, 3, 2):
        y_copy(dy).start()
    for dy in (1, 3, 2):
        y_copy(dy).wait_recv()
    terms = [y_terms[i].astype(jnp.float32) for i in range(SIDE)]
    whole = (terms[0] + terms[1]) + (terms[2] + terms[3])
    c00, c01, c10, c11 = unpack(whole[:HALF], whole[HALF:BS], whole[BS : BS + 1])
    factor = jnp.concatenate(
        [jnp.concatenate([c00, c01], axis=1), jnp.concatenate([c10, c11], axis=1)], axis=0
    )
    block = core * CLASS + z * 4 + x
    mixed, off, diagonal = pack(newton(factor, iters_ref[block]))
    inv_own[:HALF] = mixed.astype(jnp.bfloat16)
    inv_own[HALF:BS] = off.astype(jnp.bfloat16)
    inv_own[BS:] = diagonal.astype(jnp.bfloat16)

    def block_at(dz, dx):
        return core * CLASS + ((z - dz + SIDE) % SIDE) * 4 + (x - dx + SIDE) % SIDE

    def ag_copy(dz, dx):
        slot = dz * 4 + dx
        return remote(inv_own, inv_ref.at[block], ag_send.at[slot], ag_recv.at[slot], at(dx, 0, dz))

    def pass_on(dz, dx):
        slot = dz * 4 + dx
        src = inv_own if slot == 0 else inv_ref.at[block_at(dz, dx)]
        return remote(src, inv_ref.at[block_at(dz, dx)], ags_send.at[slot], ags_recv.at[slot], sibling)

    for dz, dx in plane:
        ag_copy(dz, dx).start()
    pass_on(0, 0).start()
    keep = pltpu.make_async_copy(inv_own, inv_ref.at[block], ag_send.at[0])
    keep.start()

    passed = []
    for i, (dx, dy) in enumerate([(0, 1), (0, 3), (0, 2), (2, 1), (2, 3), (2, 2)]):
        index = dy if dx == 0 else 3 + dy
        came = shard(dx, SIDE - dy)
        arrival = remote(came, came, g_send.at[index], g_recv.at[index], at(0, dy, 0))
        arrival.wait_recv()
        copy = remote(came, came, gs_send.at[2 + i], gs_recv.at[2 + i], sibling)
        copy.start()
        passed.append(copy)

    for dz, dx in plane:
        ag_copy(dz, dx).wait_recv()
        pass_on(dz, dx).start()

    mine.wait()
    keep.wait()
    first_copy.wait_send()
    for copy in g_copies + second_copies:
        copy.wait_send()
    for copy in [own_to_sib, partner_to_sib] + passed:
        copy.wait()
    for k in range(4):
        sib_copy(k).wait_send()
    for dz, dx in plane:
        rs_copy(dz, dx).wait_send()
        ag_copy(dz, dx).wait_send()
        pass_on(dz, dx).wait()
    pass_on(0, 0).wait()
    for dy in (1, 2, 3):
        y_copy(dy).wait_send()


def apply_kernel(inv_ref, grad_ref, out_ref):
    for j in range(inv_ref.shape[0]):
        packed = inv_ref[j].astype(jnp.float32)
        parts = unpack(packed[:HALF], packed[HALF:BS], packed[BS : BS + 1])
        c00, c01, c10, c11 = [part.astype(jnp.bfloat16) for part in parts]
        inverse = jnp.concatenate(
            [jnp.concatenate([c00, c01], axis=1), jnp.concatenate([c10, c11], axis=1)], axis=0
        )
        rows = grad_ref[:, j * BS : (j + 1) * BS]
        out_ref[j * BS : (j + 1) * BS] = lax.dot_general(
            inverse, rows, NT, preferred_element_type=jnp.float32
        ).astype(jnp.bfloat16)


def per_device(activations, gradient, iterations):
    width = activations.shape[1]
    columns = gradient.shape[1] * 16
    anywhere = pl.BlockSpec(memory_space=pl.ANY)
    dma = pltpu.SemaphoreType.DMA
    full, inverses = pl.pallas_call(
        factor_kernel,
        name="factor",
        out_shape=[
            jax.ShapeDtypeStruct((columns, width), jnp.bfloat16),
            jax.ShapeDtypeStruct((BLOCKS, PACK, HALF), jnp.bfloat16),
        ],
        in_specs=[anywhere, anywhere, pl.BlockSpec(memory_space=pltpu.SMEM)],
        out_specs=[anywhere, anywhere],
        scratch_shapes=[
            pltpu.VMEM((8, activations.shape[0], GROUP_COLS), jnp.bfloat16),
            pltpu.VMEM((4, GROUP, PACK, HALF), jnp.bfloat16),
            pltpu.VMEM((4, GROUP, PACK, HALF), jnp.bfloat16),
            pltpu.VMEM((GROUP, PACK, HALF), jnp.float32),
            pltpu.VMEM((4, GROUP, PACK, HALF), jnp.bfloat16),
            pltpu.VMEM((16, PACK, HALF), jnp.bfloat16),
            pltpu.VMEM((SIDE, PACK, HALF), jnp.bfloat16),
            pltpu.VMEM((PACK, HALF), jnp.bfloat16),
            dma((8,)), dma((4,)), dma((4,)), dma((16,)), dma((16,)), dma((4,)), dma((4,)),
            dma((16,)), dma((16,)), dma((16,)), dma((16,)),
            dma, dma((7,)), dma((7,)), dma((8,)), dma((8,)),
        ],
        compiler_params=pltpu.CompilerParams(
            collective_id=0, has_side_effects=True, vmem_limit_bytes=48 << 20
        ),
        cost_estimate=pl.CostEstimate(flops=5 * 10**9, bytes_accessed=32 << 20, transcendentals=0),
    )(activations, gradient.T, iterations)
    step = 4
    return pl.pallas_call(
        apply_kernel,
        name="apply",
        grid=(BLOCKS // step,),
        out_shape=jax.ShapeDtypeStruct((width, columns), jnp.bfloat16),
        in_specs=[
            pl.BlockSpec((step, PACK, HALF), lambda i: (i, 0, 0)),
            pl.BlockSpec((columns, step * BS), lambda i: (0, i)),
        ],
        out_specs=pl.BlockSpec((step * BS, columns), lambda i: (i, 0)),
        compiler_params=pltpu.CompilerParams(vmem_limit_bytes=32 << 20),
        cost_estimate=pl.CostEstimate(flops=2 * 10**9, bytes_accessed=20 << 20, transcendentals=0),
    )(inverses, full)


def solution(mesh):
    placed = (P(("dp", "owner"), None), P(None, ("dp", "owner")), P())
    return jax.shard_map(
        per_device, mesh=mesh, in_specs=placed, out_specs=P(None, "dp"), check_vma=False
    )
```

```python
import functools

import jax
import jax.numpy as jnp
from jax import lax
from jax.experimental import pallas as pl
from jax.experimental.pallas import tpu as pltpu
from jax.sharding import PartitionSpec as P

BS = 256
HALF = BS // 2
BLOCKS = 32
PACK = BS + 16
PART = 144
PACK_INV = 2 * PART
TOKENS = 131072
DAMPING = 0.1
ITERS = 8
LEAST_ITERS = 5
SIDE = 4
GROUP = 4
GROUP_COLS = GROUP * BS
CLASS = 16
AHEAD = 3
MESH = pl.DeviceIdType.MESH

TN = (((0,), (0,)), ((), ()))
NT = (((1,), (1,)), ((), ()))


def here():
    shard = lax.axis_index("dp")
    owner = lax.axis_index("owner")
    x = (owner // 8) * 2 + shard % 2
    return x, (owner // 2) % 4, shard // 2, owner % 2


def mesh_id(x, y, z, core):
    return (z * 2 + x % 2, (x // 2) * 8 + y * 2 + core)


def owner_of(x, y, core):
    return (x // 2) * 8 + y * 2 + core


def tile_iota():
    rows = lax.broadcasted_iota(jnp.int32, (HALF, HALF), 0)
    cols = lax.broadcasted_iota(jnp.int32, (HALF, HALF), 1)
    return rows, cols


def pack(block):
    rows, cols = tile_iota()
    low = block[HALF:, HALF:]
    mixed = jnp.where(rows <= cols, block[:HALF, :HALF], low)
    diagonal = jnp.sum(jnp.where(rows == cols, low, 0.0), axis=0, keepdims=True)
    return mixed, block[:HALF, HALF:], jnp.broadcast_to(diagonal, (16, HALF))


def unpack(mixed, off, diagonal):
    rows, cols = tile_iota()
    turned = mixed.T
    first = jnp.where(rows <= cols, mixed, turned)
    second = jnp.where(rows > cols, mixed, jnp.where(rows < cols, turned, diagonal))
    return first, off, off.T, second


def split(value):
    high = value.astype(jnp.bfloat16)
    return high, (value - high.astype(jnp.float32)).astype(jnp.bfloat16)


def dot3(left, right):
    lh, ll = split(left)
    rh, rl = split(right)
    mul = functools.partial(jnp.dot, preferred_element_type=jnp.float32)
    return mul(lh, rh) + (mul(lh, rl) + mul(ll, rh))


def newton(factor, count):
    rows = lax.broadcasted_iota(jnp.int32, (BS, BS), 0)
    cols = lax.broadcasted_iota(jnp.int32, (BS, BS), 1)
    identity = jnp.where(rows == cols, 1.0, 0.0)
    damped = factor / TOKENS + DAMPING * identity
    bound = jnp.max(jnp.sum(jnp.abs(damped), axis=1))
    ratio = damped / bound
    approx = (2.0 * identity - ratio) / bound
    ratio = 2.0 * ratio - dot3(ratio, ratio)
    for step in range(1, ITERS):
        if step < ITERS - 1:
            both = dot3(jnp.concatenate([ratio, approx], axis=0), ratio)
            later = 2.0 * approx - both[BS:]
            ratio = 2.0 * ratio - both[:BS]
        else:
            later = 2.0 * approx - dot3(approx, ratio)
        approx = later if step < LEAST_ITERS else jnp.where(step < count, later, approx)
    return approx


def factor_kernel(
    act_ref, grad_ref, iters_ref,
    full_ref, inv_ref,
    act, to_sib, from_sib, own, summed, landed, y_terms, inv_own, count,
    act_sem, sib_send, sib_recv, rs_send, rs_recv, y_send, y_recv,
    ag_send, ag_recv, agy_send, agy_recv, ags_send, ags_recv,
    local_sem, g_send, g_recv, gs_send, gs_recv,
):
    x, y, z, core = here()
    sibling = mesh_id(x, y, z, 1 - core)

    def at(dx, dy, dz):
        return mesh_id((x + dx) % SIDE, (y + dy) % SIDE, (z + dz) % SIDE, core)

    plane = [(dz, dx) for dz in (1, 2, 3, 0) for dx in range(SIDE) if dz or dx]

    def remote(src, dst, send, recv, target):
        return pltpu.make_async_remote_copy(
            src_ref=src, dst_ref=dst, send_sem=send, recv_sem=recv, device_id=target, device_id_type=MESH
        )

    def act_copy(slot):
        side = 1 - core if slot % 2 == 0 else core
        group = side * 4 + (z + slot // 2 + 1) % SIDE
        cols = pl.ds(pl.multiple_of(group * GROUP_COLS, GROUP_COLS), GROUP_COLS)
        return pltpu.make_async_copy(act_ref.at[:, cols], act.at[slot], act_sem.at[slot])

    for slot in range(AHEAD):
        act_copy(slot).start()
    counts = pltpu.make_async_copy(iters_ref, count, local_sem.at[2])
    counts.start()

    barrier = pltpu.get_barrier_semaphore()
    partners = [sibling] + [at(dx, 0, dz) for dz, dx in plane] + [at(0, dy, 0) for dy in (1, 2, 3)]
    for partner in partners:
        pl.semaphore_signal(barrier, inc=1, device_id=partner, device_id_type=MESH)
    pl.semaphore_wait(barrier, len(partners))

    def rows_of(dx, dy, first, rows):
        start = owner_of((x + dx) % SIDE, (y + dy) % SIDE, core) * 32 + first
        return full_ref.at[pl.ds(pl.multiple_of(start, 16), rows)]

    def shard(dx, dy):
        return rows_of(dx, dy, 0, 32)

    mine = pltpu.make_async_copy(grad_ref, shard(0, 0), local_sem.at[0])
    mine.start()

    def gather_copy(src, dst, index, dx, dy):
        return remote(src, dst, g_send.at[index], g_recv.at[index], at(dx, dy, 0))

    own_out = [
        gather_copy(grad_ref, shard(0, 0), 0, 0, 1),
        gather_copy(grad_ref, shard(0, 0), 1, 0, 3),
        gather_copy(grad_ref, shard(0, 0), 2, 2, 0),
    ]
    for copy in own_out:
        copy.start()

    def arrived(index, place):
        gather_copy(place, place, index, 0, 1).wait_recv()

    def sib_shard(index, place, src=None):
        copy = remote(place if src is None else src, place, gs_send.at[index], gs_recv.at[index], sibling)
        copy.start()
        return copy

    to_sibling = [sib_shard(0, shard(0, 0), grad_ref)]

    def products(slot, store):
        act_copy(slot).wait()
        if slot + AHEAD < 8:
            act_copy(slot + AHEAD).start()
        for j in range(GROUP):
            cols = act[slot, :, j * BS : (j + 1) * BS]
            mixed, off, diagonal = pack(lax.dot_general(cols, cols, TN, preferred_element_type=jnp.float32))
            store(j, 0, HALF, mixed)
            store(j, HALF, HALF, off)
            store(j, BS, 16, diagonal)

    def sib_copy(k):
        return remote(to_sib.at[k], from_sib.at[k], sib_send.at[k], sib_recv.at[k], sibling)

    def rs_copy(dz, dx):
        k = (dz + 3) % 4
        slot = dz * 4 + dx
        return remote(
            summed.at[k, (x + dx) % SIDE], landed.at[slot], rs_send.at[slot], rs_recv.at[slot], at(dx, 0, dz)
        )

    for k in range(4):

        def store_sib(j, first, rows, value):
            to_sib[k, j, first : first + rows] = value.astype(jnp.bfloat16)

        def store_own(j, first, rows, value):
            own[j, first : first + rows] = value

        products(2 * k, store_sib)
        sib_copy(k).start()
        products(2 * k + 1, store_own)
        sib_copy(k).wait_recv()
        summed[k] = (own[...] + from_sib[k].astype(jnp.float32)).astype(jnp.bfloat16)
        for dx in range(SIDE):
            if k < 3 or dx:
                rs_copy((k + 1) % 4, dx).start()

    arrived(2, shard(2, 0))
    second = [gather_copy(shard(2, 0), shard(2, 0), 3, 0, 1), gather_copy(shard(2, 0), shard(2, 0), 4, 0, 3)]
    for copy in second:
        copy.start()
    arrived(0, shard(0, 3))
    arrived(1, shard(0, 1))
    halves = [
        gather_copy(rows_of(0, 3, 0, 16), rows_of(0, 3, 0, 16), 5, 0, 1),
        gather_copy(rows_of(0, 1, 16, 16), rows_of(0, 1, 16, 16), 6, 0, 3),
    ]
    for copy in halves:
        copy.start()
    second += halves
    to_sibling += [sib_shard(1, shard(2, 0)), sib_shard(2, shard(0, 3)), sib_shard(3, shard(0, 1))]

    total = summed[3, pl.ds(x, 1)][0].astype(jnp.float32)
    for dz, dx in plane:
        rs_copy(dz, dx).wait_recv()
        total = total + landed[dz * 4 + dx].astype(jnp.float32)
    y_terms[pl.ds(y, 1)] = total.astype(jnp.bfloat16)[None]

    def y_copy(dy):
        return remote(y_terms.at[y], y_terms.at[y], y_send.at[dy], y_recv.at[dy], at(0, dy, 0))

    for dy in (1, 3, 2):
        y_copy(dy).start()
    for dy in (1, 3, 2):
        y_copy(dy).wait_recv()
    terms = [y_terms[i].astype(jnp.float32) for i in range(SIDE)]
    whole = (terms[0] + terms[1]) + (terms[2] + terms[3])
    c00, c01, c10, c11 = unpack(whole[:HALF], whole[HALF:BS], whole[BS : BS + 1])
    factor = jnp.concatenate(
        [jnp.concatenate([c00, c01], axis=1), jnp.concatenate([c10, c11], axis=1)], axis=0
    )
    block = core * CLASS + z * 4 + x
    counts.wait()
    mixed, off, diagonal = pack(newton(factor, count[block]))
    inv_own[:HALF] = mixed.astype(jnp.bfloat16)
    inv_own[HALF:BS] = off.astype(jnp.bfloat16)
    inv_own[BS:PACK] = diagonal.astype(jnp.bfloat16)
    inv_own[PACK:] = jnp.zeros((PACK_INV - PACK, HALF), jnp.bfloat16)

    held = pl.ds(pl.multiple_of((y % 2) * PART, PART), PART)
    other = pl.ds(pl.multiple_of((1 - y % 2) * PART, PART), PART)

    def place(dz, dx, part):
        return inv_ref.at[core * CLASS + ((z - dz + SIDE) % SIDE) * 4 + (x - dx + SIDE) % SIDE, part]

    def ag_copy(dz, dx):
        slot = dz * 4 + dx
        return remote(inv_own.at[held], place(0, 0, held), ag_send.at[slot], ag_recv.at[slot], at(dx, 0, dz))

    def trade(dz, dx, part):
        slot = dz * 4 + dx
        dy = 1 if dx < 2 else 3
        return remote(place(dz, dx, part), place(dz, dx, part), agy_send.at[slot], agy_recv.at[slot], at(0, dy, 0))

    def pass_on(dz, dx, part, which):
        slot = dz * 4 + dx + 16 * which
        src = inv_own.at[part] if dz == 0 and dx == 0 else place(dz, dx, part)
        return remote(src, place(dz, dx, part), ags_send.at[slot], ags_recv.at[slot], sibling)

    for dz, dx in plane:
        ag_copy(dz, dx).start()
    whole_rows = pl.ds(0, PACK_INV)
    pass_on(0, 0, whole_rows, 0).start()
    keep = pltpu.make_async_copy(inv_own, place(0, 0, whole_rows), local_sem.at[1])
    keep.start()

    arrived(3, shard(2, 3))
    arrived(4, shard(2, 1))
    third = [
        gather_copy(rows_of(2, 3, 0, 16), rows_of(2, 3, 0, 16), 7, 0, 1),
        gather_copy(rows_of(2, 1, 16, 16), rows_of(2, 1, 16, 16), 8, 0, 3),
    ]
    for copy in third:
        copy.start()
    to_sibling += [sib_shard(4, shard(2, 3)), sib_shard(5, shard(2, 1))]
    arrived(5, rows_of(0, 2, 0, 16))
    arrived(6, rows_of(0, 2, 16, 16))
    to_sibling += [sib_shard(6, shard(0, 2))]

    for dz, dx in plane:
        ag_copy(dz, dx).wait_recv()
        trade(dz, dx, held).start()
        pass_on(dz, dx, held, 0).start()
    for dz, dx in plane:
        trade(dz, dx, other).wait_recv()
        pass_on(dz, dx, other, 1).start()
    arrived(7, rows_of(2, 2, 0, 16))
    arrived(8, rows_of(2, 2, 16, 16))
    to_sibling += [sib_shard(7, shard(2, 2))]

    mine.wait()
    keep.wait()
    for copy in own_out + second + third:
        copy.wait_send()
    for k in range(4):
        sib_copy(k).wait_send()
    for dz, dx in plane:
        rs_copy(dz, dx).wait_send()
        ag_copy(dz, dx).wait_send()
        trade(dz, dx, held).wait_send()
        pass_on(dz, dx, held, 0).wait()
        pass_on(dz, dx, other, 1).wait()
    pass_on(0, 0, whole_rows, 0).wait()
    for dy in (1, 2, 3):
        y_copy(dy).wait_send()
    for copy in to_sibling:
        copy.wait()


def apply_kernel(inv_ref, grad_ref, out_ref):
    for j in range(inv_ref.shape[0]):
        packed = inv_ref[j].astype(jnp.float32)
        parts = unpack(packed[:HALF], packed[HALF:BS], packed[BS : BS + 1])
        c00, c01, c10, c11 = [part.astype(jnp.bfloat16) for part in parts]
        inverse = jnp.concatenate(
            [jnp.concatenate([c00, c01], axis=1), jnp.concatenate([c10, c11], axis=1)], axis=0
        )
        rows = grad_ref[:, j * BS : (j + 1) * BS]
        out_ref[j * BS : (j + 1) * BS] = lax.dot_general(
            inverse, rows, NT, preferred_element_type=jnp.float32
        ).astype(jnp.bfloat16)


def per_device(activations, gradient, iterations):
    width = activations.shape[1]
    columns = gradient.shape[1] * 16
    anywhere = pl.BlockSpec(memory_space=pl.ANY)
    hbm = pl.BlockSpec(memory_space=pltpu.HBM)
    dma = pltpu.SemaphoreType.DMA
    full, inverses = pl.pallas_call(
        factor_kernel,
        name="factor",
        out_shape=[
            jax.ShapeDtypeStruct((columns, width), jnp.bfloat16),
            jax.ShapeDtypeStruct((BLOCKS, PACK_INV, HALF), jnp.bfloat16),
        ],
        in_specs=[hbm, hbm, hbm],
        out_specs=[anywhere, anywhere],
        scratch_shapes=[
            pltpu.VMEM((8, activations.shape[0], GROUP_COLS), jnp.bfloat16),
            pltpu.VMEM((4, GROUP, PACK, HALF), jnp.bfloat16),
            pltpu.VMEM((4, GROUP, PACK, HALF), jnp.bfloat16),
            pltpu.VMEM((GROUP, PACK, HALF), jnp.float32),
            pltpu.VMEM((4, GROUP, PACK, HALF), jnp.bfloat16),
            pltpu.VMEM((16, PACK, HALF), jnp.bfloat16),
            pltpu.VMEM((SIDE, PACK, HALF), jnp.bfloat16),
            pltpu.VMEM((PACK_INV, HALF), jnp.bfloat16),
            pltpu.SMEM((BLOCKS,), jnp.int32),
            dma((8,)), dma((4,)), dma((4,)), dma((16,)), dma((16,)), dma((4,)), dma((4,)),
            dma((16,)), dma((16,)), dma((16,)), dma((16,)), dma((32,)), dma((32,)),
            dma((3,)), dma((9,)), dma((9,)), dma((8,)), dma((8,)),
        ],
        compiler_params=pltpu.CompilerParams(
            collective_id=0, has_side_effects=True, vmem_limit_bytes=32 << 20
        ),
        cost_estimate=pl.CostEstimate(flops=5 * 10**9, bytes_accessed=32 << 20, transcendentals=0),
    )(activations, gradient.T, iterations)
    step = 4
    return pl.pallas_call(
        apply_kernel,
        name="apply",
        grid=(BLOCKS // step,),
        out_shape=jax.ShapeDtypeStruct((width, columns), jnp.bfloat16),
        in_specs=[
            pl.BlockSpec((step, PACK_INV, HALF), lambda i: (i, 0, 0)),
            pl.BlockSpec((columns, step * BS), lambda i: (0, i)),
        ],
        out_specs=pl.BlockSpec((step * BS, columns), lambda i: (i, 0)),
        compiler_params=pltpu.CompilerParams(vmem_limit_bytes=32 << 20),
        cost_estimate=pl.CostEstimate(flops=2 * 10**9, bytes_accessed=20 << 20, transcendentals=0),
    )(inverses, full)


def solution(mesh):
    placed = (P(("dp", "owner"), None), P(None, ("dp", "owner")), P())
    return jax.shard_map(
        per_device, mesh=mesh, in_specs=placed, out_specs=P(None, "dp"), check_vma=False
    )
```

```python
import functools

import jax
import jax.numpy as jnp
from jax import lax
from jax.experimental import pallas as pl
from jax.experimental.pallas import tpu as pltpu
from jax.sharding import PartitionSpec as P

BS = 256
HALF = BS // 2
BLOCKS = 32
PACK = BS + 16
PART = 144
PACK_INV = 2 * PART
TOKENS = 131072
DAMPING = 0.1
ITERS = 8
LEAST_ITERS = 5
SIDE = 4
GROUP = 4
GROUP_COLS = GROUP * BS
CLASS = 16
AHEAD = 4
AWAY = (2, 1, 3, 0)
X_EARLY = 4096
Y_EARLY = 2048
ACROSS = 4096
S2_FIRST = False
MESH = pl.DeviceIdType.MESH

TN = (((0,), (0,)), ((), ()))
NT = (((1,), (1,)), ((), ()))


def here():
    shard = lax.axis_index("dp")
    owner = lax.axis_index("owner")
    x = (owner // 8) * 2 + shard % 2
    return x, (owner // 2) % 4, shard // 2, owner % 2


def mesh_id(x, y, z, core):
    return (z * 2 + x % 2, (x // 2) * 8 + y * 2 + core)


def owner_of(x, y, core):
    return (x // 2) * 8 + y * 2 + core


def tile_iota():
    rows = lax.broadcasted_iota(jnp.int32, (HALF, HALF), 0)
    cols = lax.broadcasted_iota(jnp.int32, (HALF, HALF), 1)
    return rows, cols


def pack(block):
    rows, cols = tile_iota()
    low = block[HALF:, HALF:]
    mixed = jnp.where(rows <= cols, block[:HALF, :HALF], low)
    diagonal = jnp.sum(jnp.where(rows == cols, low, 0.0), axis=0, keepdims=True)
    return mixed, block[:HALF, HALF:], jnp.broadcast_to(diagonal, (16, HALF))


def unpack(mixed, off, diagonal):
    rows, cols = tile_iota()
    turned = mixed.T
    first = jnp.where(rows <= cols, mixed, turned)
    second = jnp.where(rows > cols, mixed, jnp.where(rows < cols, turned, diagonal))
    return first, off, off.T, second


def split(value):
    high = value.astype(jnp.bfloat16)
    return high, (value - high.astype(jnp.float32)).astype(jnp.bfloat16)


def dot3(left, right):
    lh, ll = split(left)
    rh, rl = split(right)
    mul = functools.partial(jnp.dot, preferred_element_type=jnp.float32)
    return mul(lh, rh) + (mul(lh, rl) + mul(ll, rh))


def newton(factor, count):
    rows = lax.broadcasted_iota(jnp.int32, (BS, BS), 0)
    cols = lax.broadcasted_iota(jnp.int32, (BS, BS), 1)
    identity = jnp.where(rows == cols, 1.0, 0.0)
    damped = factor / TOKENS + DAMPING * identity
    bound = jnp.max(jnp.sum(jnp.abs(damped), axis=1))
    ratio = damped / bound
    approx = (2.0 * identity - ratio) / bound
    ratio = 2.0 * ratio - dot3(ratio, ratio)
    for step in range(1, ITERS):
        if step < ITERS - 1:
            both = dot3(jnp.concatenate([ratio, approx], axis=0), ratio)
            later = 2.0 * approx - both[BS:]
            ratio = 2.0 * ratio - both[:BS]
        else:
            later = 2.0 * approx - dot3(approx, ratio)
        approx = later if step < LEAST_ITERS else jnp.where(step < count, later, approx)
    return approx


def factor_kernel(
    act_ref, grad_ref, iters_ref,
    full_ref, inv_ref,
    act, to_sib, from_sib, own, summed, z_land, x_land, x_terms, z_terms, x_last, z_last, y_terms, inv_own, count,
    act_sem, sib_send, sib_recv, z_send, z_recv, x_send, x_recv, y_send, y_recv, x2_send, x2_recv, z2_send, z2_recv,
    agx_send, agx_recv, agz_send, agz_recv, agx2_send, agx2_recv, agz2_send, agz2_recv, ags_send, ags_recv,
    local_sem, g_send, g_recv, gs_send, gs_recv,
):
    x, y, z, core = here()
    sibling = mesh_id(x, y, z, 1 - core)

    def at(dx, dy, dz):
        return mesh_id((x + dx) % SIDE, (y + dy) % SIDE, (z + dz) % SIDE, core)

    def remote(src, dst, send, recv, target):
        return pltpu.make_async_remote_copy(
            src_ref=src, dst_ref=dst, send_sem=send, recv_sem=recv, device_id=target, device_id_type=MESH
        )

    work = [("sib", 0), ("sib", 1), ("own", 0), ("sib", 2), ("own", 1), ("sib", 3), ("own", 2), ("own", 3)]

    def act_copy(slot):
        kind, k = work[slot]
        side = 1 - core if kind == "sib" else core
        group = side * 4 + (z + AWAY[k]) % SIDE
        cols = pl.ds(pl.multiple_of(group * GROUP_COLS, GROUP_COLS), GROUP_COLS)
        return pltpu.make_async_copy(act_ref.at[:, cols], act.at[slot], act_sem.at[slot])

    for slot in range(AHEAD):
        act_copy(slot).start()
    counts = pltpu.make_async_copy(iters_ref, count, local_sem.at[2])
    counts.start()

    barrier = pltpu.get_barrier_semaphore()
    partners = [sibling]
    for d in (1, 2, 3):
        partners += [at(0, d, 0), at(d, 0, 0), at(0, 0, d)]
    for partner in partners:
        pl.semaphore_signal(barrier, inc=1, device_id=partner, device_id_type=MESH)

    def products(slot, store):
        act_copy(slot).wait()
        if slot + AHEAD < 8:
            act_copy(slot + AHEAD).start()
        for j in range(GROUP):
            cols = act[slot, :, j * BS : (j + 1) * BS]
            mixed, off, diagonal = pack(lax.dot_general(cols, cols, TN, preferred_element_type=jnp.float32))
            store(j, 0, HALF, mixed)
            store(j, HALF, HALF, off)
            store(j, BS, 16, diagonal)

    def sib_products(slot):
        k = work[slot][1]

        def store(j, first, rows, value):
            to_sib[k, j, first : first + rows] = value.astype(jnp.bfloat16)

        products(slot, store)

    sib_products(0)
    pl.semaphore_wait(barrier, len(partners))

    def rows_of(dx, dy, first, rows, cols=slice(None)):
        start = owner_of((x + dx) % SIDE, (y + dy) % SIDE, core) * 32 + first
        return full_ref.at[pl.ds(pl.multiple_of(start, 16), rows), cols]

    def shard(dx, dy):
        return rows_of(dx, dy, 0, 32)

    mine = pltpu.make_async_copy(grad_ref, shard(0, 0), local_sem.at[0])
    mine.start()
    gathers = []

    def gather(index, dx, dy, place, src=None):
        copy = remote(place if src is None else src, place, g_send.at[index], g_recv.at[index], at(dx, dy, 0))
        copy.start()
        gathers.append(copy)

    def arrived(index, place):
        remote(place, place, g_send.at[index], g_recv.at[index], at(0, 1, 0)).wait_recv()

    passes = []

    def to_sibling(index, place, src=None):
        copy = remote(place if src is None else src, place, gs_send.at[index], gs_recv.at[index], sibling)
        copy.start()
        passes.append(copy)

    def columns(first, last):
        return pl.ds(first, last - first)

    def send_parts(index, dx, dy, first, last, src=None):
        cols = columns(first, last)
        gather(index, dx, dy, rows_of(0, 0, 0, 32, cols) if src is None else src, grad_ref.at[:, cols] if src is None else None)

    width = grad_ref.shape[1]
    gather(0, 0, 1, shard(0, 0), grad_ref)
    gather(1, 0, 3, shard(0, 0), grad_ref)
    send_parts(2, 2, 0, 0, X_EARLY)

    def sib_copy(k):
        return remote(to_sib.at[k], from_sib.at[k], sib_send.at[k], sib_recv.at[k], sibling)

    def z_copy(k):
        return remote(summed.at[k, :, :PART], z_land.at[k], z_send.at[k], z_recv.at[k], at(0, 0, AWAY[k]))

    def x_copy(dx, k):
        return remote(
            summed.at[k : k + 2, (x + dx) % SIDE, PART:], x_land.at[dx, k : k + 2],
            x_send.at[dx, k // 2], x_recv.at[dx, k // 2], at(dx, 0, 0),
        )

    sib_copy(0).start()
    for slot in range(1, 8):
        kind, k = work[slot]
        if kind == "sib":
            sib_products(slot)
            sib_copy(k).start()
            continue

        def store_own(j, first, rows, value):
            own[j, first : first + rows] = value

        products(slot, store_own)
        sib_copy(k).wait_recv()
        summed[k] = (own[...] + from_sib[k].astype(jnp.float32)).astype(jnp.bfloat16)
        if k < 3:
            z_copy(k).start()
        if k % 2:
            for dx in (2, 1, 3):
                x_copy(dx, k - 1).start()

    to_sibling(0, shard(0, 0), grad_ref)

    totals = own[:, :PART] + from_sib[3, :, :PART].astype(jnp.float32)
    for k in range(3):
        z_copy(k).wait_recv()
        totals = totals + z_land[k].astype(jnp.float32)
    x_terms[...] = totals.astype(jnp.bfloat16)

    def x_copy2(dx):
        return remote(x_terms.at[(x + dx) % SIDE], x_last.at[dx], x2_send.at[dx], x2_recv.at[dx], at(dx, 0, 0))

    def z_copy2(k):
        return remote(z_terms.at[k], z_last.at[k], z2_send.at[k], z2_recv.at[k], at(0, 0, AWAY[k]))

    for dx in (2, 1, 3):
        x_copy2(dx).start()
    for half in (0, 2):
        for dx in (1, 3, 2):
            x_copy(dx, half).wait_recv()
        for k in (half, half + 1):
            mine_here = summed[k, pl.ds(x, 1), PART:][0].astype(jnp.float32)
            for dx in (1, 3, 2):
                mine_here = mine_here + x_land[dx, k].astype(jnp.float32)
            z_terms[k] = mine_here.astype(jnp.bfloat16)
            if k < 3:
                z_copy2(k).start()

    if X_EARLY < width:
        send_parts(3, 2, 0, X_EARLY, width)
    arrived(2, rows_of(2, 0, 0, 32, columns(0, X_EARLY)))
    if Y_EARLY:
        send_parts(4, 0, 1, 0, Y_EARLY, rows_of(2, 0, 0, 32, columns(0, Y_EARLY)))
        send_parts(5, 0, 3, 0, Y_EARLY, rows_of(2, 0, 0, 32, columns(0, Y_EARLY)))

    first = x_terms[pl.ds(x, 1)][0].astype(jnp.float32)
    for dx in (1, 3, 2):
        x_copy2(dx).wait_recv()
        first = first + x_last[dx].astype(jnp.float32)
    rest = z_terms[3].astype(jnp.float32)
    for k in (1, 2, 0):
        z_copy2(k).wait_recv()
        rest = rest + z_last[k].astype(jnp.float32)
    y_terms[pl.ds(y, 1), :PART] = first.astype(jnp.bfloat16)[None]
    y_terms[pl.ds(y, 1), PART:] = rest.astype(jnp.bfloat16)[None]

    def y_copy(dy):
        return remote(y_terms.at[y], y_terms.at[y], y_send.at[dy], y_recv.at[dy], at(0, dy, 0))

    def send_opposite():
        arrived(6, rows_of(0, 2, 0, 16))
        arrived(7, rows_of(0, 2, 16, 16))
        if ACROSS:
            gather(10, 2, 0, rows_of(0, 2, 0, 32, columns(0, ACROSS)))
        to_sibling(4, shard(0, 2))

    for dy in (2, 1, 3):
        y_copy(dy).start()

    arrived(0, shard(0, 3))
    gather(6, 0, 1, rows_of(0, 3, 0, 16))
    arrived(1, shard(0, 1))
    gather(7, 0, 3, rows_of(0, 1, 16, 16))
    to_sibling(1, shard(0, 3))
    to_sibling(2, shard(0, 1))
    for dy in (1, 3, 2):
        y_copy(dy).wait_recv()

    if X_EARLY < width:
        arrived(3, rows_of(2, 0, 0, 32, columns(X_EARLY, width)))
    send_parts(8, 0, 1, Y_EARLY, width, rows_of(2, 0, 0, 32, columns(Y_EARLY, width)))
    send_parts(9, 0, 3, Y_EARLY, width, rows_of(2, 0, 0, 32, columns(Y_EARLY, width)))
    to_sibling(3, shard(2, 0))
    if S2_FIRST:
        send_opposite()

    terms = [y_terms[i].astype(jnp.float32) for i in range(SIDE)]
    whole = (terms[0] + terms[1]) + (terms[2] + terms[3])
    c00, c01, c10, c11 = unpack(whole[:HALF], whole[HALF:BS], whole[BS : BS + 1])
    factor = jnp.concatenate(
        [jnp.concatenate([c00, c01], axis=1), jnp.concatenate([c10, c11], axis=1)], axis=0
    )
    block = core * CLASS + z * 4 + x
    counts.wait()
    mixed, off, diagonal = pack(newton(factor, count[block]))
    inv_own[:HALF] = mixed.astype(jnp.bfloat16)
    inv_own[HALF:BS] = off.astype(jnp.bfloat16)
    inv_own[BS:PACK] = diagonal.astype(jnp.bfloat16)
    inv_own[PACK:] = jnp.zeros((PACK_INV - PACK, HALF), jnp.bfloat16)

    upper, lower = pl.ds(0, PART), pl.ds(PART, PART)

    def agx_copy(d):
        return remote(inv_own.at[upper], inv_ref.at[core, z, x, upper], agx_send.at[d], agx_recv.at[d], at(d, 0, 0))

    def agz_copy(d):
        return remote(inv_own.at[lower], inv_ref.at[core, z, x, lower], agz_send.at[d], agz_recv.at[d], at(0, 0, d))

    def along_x(d):
        return inv_ref.at[core, (z + SIDE - d) % SIDE, :, upper]

    def along_z(d):
        return inv_ref.at[core, :, (x + SIDE - d) % SIDE, lower]

    def agz_copy2(d):
        return remote(along_x(0), along_x(0), agz2_send.at[d], agz2_recv.at[d], at(0, 0, d))

    def agx_copy2(d):
        return remote(along_z(0), along_z(0), agx2_send.at[d], agx2_recv.at[d], at(d, 0, 0))

    def pass_on(place, slot):
        return remote(place, place, ags_send.at[slot], ags_recv.at[slot], sibling)

    for d in (2, 1, 3):
        agx_copy(d).start()
        agz_copy(d).start()
    keep = pltpu.make_async_copy(inv_own, inv_ref.at[core, z, x], local_sem.at[1])
    keep.start()
    keep.wait()
    for d in (1, 3, 2):
        agx_copy(d).wait_recv()
    for d in (2, 1, 3):
        agz_copy2(d).start()
    for d in (1, 3, 2):
        agz_copy(d).wait_recv()
    for d in (2, 1, 3):
        agx_copy2(d).start()
    pass_on(along_x(0), 0).start()
    pass_on(along_z(0), 4).start()
    if not S2_FIRST:
        send_opposite()
    for dy, one, two in ((3, 4, 8), (1, 5, 9)):
        if Y_EARLY:
            arrived(one, rows_of(2, dy, 0, 32, columns(0, Y_EARLY)))
        arrived(two, rows_of(2, dy, 0, 32, columns(Y_EARLY, width)))
        if ACROSS < width:
            first_row = 0 if dy == 3 else 16
            gather(11 + first_row // 16, 0, 4 - dy, rows_of(2, dy, first_row, 16, columns(ACROSS, width)))
        to_sibling(5 + first_row // 16 if ACROSS < width else 5 + dy // 2, shard(2, dy))
    for d in (1, 3, 2):
        agz_copy2(d).wait_recv()
        pass_on(along_x(d), d).start()
        agx_copy2(d).wait_recv()
        pass_on(along_z(d), 4 + d).start()
    if ACROSS:
        arrived(10, rows_of(2, 2, 0, 32, columns(0, ACROSS)))
    if ACROSS < width:
        arrived(11, rows_of(2, 2, 0, 16, columns(ACROSS, width)))
        arrived(12, rows_of(2, 2, 16, 16, columns(ACROSS, width)))
    to_sibling(7, shard(2, 2))

    mine.wait()
    for copy in gathers:
        copy.wait_send()
    for k in range(4):
        sib_copy(k).wait_send()
    for k in range(3):
        z_copy(k).wait_send()
        z_copy2(k).wait_send()
    for d in (1, 2, 3):
        x_copy(d, 0).wait_send()
        x_copy(d, 2).wait_send()
        x_copy2(d).wait_send()
        y_copy(d).wait_send()
        agx_copy(d).wait_send()
        agz_copy(d).wait_send()
        agx_copy2(d).wait_send()
        agz_copy2(d).wait_send()
    for d in range(4):
        pass_on(along_x(d), d).wait()
        pass_on(along_z(d), 4 + d).wait()
    for copy in passes:
        copy.wait()


def apply_kernel(inv_ref, grad_ref, out_ref):
    for j in range(inv_ref.shape[0]):
        packed = inv_ref[j].astype(jnp.float32)
        parts = unpack(packed[:HALF], packed[HALF:BS], packed[BS : BS + 1])
        c00, c01, c10, c11 = [part.astype(jnp.bfloat16) for part in parts]
        inverse = jnp.concatenate(
            [jnp.concatenate([c00, c01], axis=1), jnp.concatenate([c10, c11], axis=1)], axis=0
        )
        rows = grad_ref[:, j * BS : (j + 1) * BS]
        out_ref[j * BS : (j + 1) * BS] = lax.dot_general(
            inverse, rows, NT, preferred_element_type=jnp.float32
        ).astype(jnp.bfloat16)


def per_device(activations, gradient, iterations):
    width = activations.shape[1]
    columns = gradient.shape[1] * 16
    anywhere = pl.BlockSpec(memory_space=pl.ANY)
    hbm = pl.BlockSpec(memory_space=pltpu.HBM)
    dma = pltpu.SemaphoreType.DMA
    full, inverses = pl.pallas_call(
        factor_kernel,
        name="factor",
        out_shape=[
            jax.ShapeDtypeStruct((columns, width), jnp.bfloat16),
            jax.ShapeDtypeStruct((2, SIDE, SIDE, PACK_INV, HALF), jnp.bfloat16),
        ],
        in_specs=[hbm, hbm, hbm],
        out_specs=[anywhere, anywhere],
        scratch_shapes=[
            pltpu.VMEM((8, activations.shape[0], GROUP_COLS), jnp.bfloat16),
            pltpu.VMEM((4, GROUP, PACK, HALF), jnp.bfloat16),
            pltpu.VMEM((4, GROUP, PACK, HALF), jnp.bfloat16),
            pltpu.VMEM((GROUP, PACK, HALF), jnp.float32),
            pltpu.VMEM((4, GROUP, PACK, HALF), jnp.bfloat16),
            pltpu.VMEM((3, GROUP, PART, HALF), jnp.bfloat16),
            pltpu.VMEM((SIDE, 4, PACK - PART, HALF), jnp.bfloat16),
            pltpu.VMEM((GROUP, PART, HALF), jnp.bfloat16),
            pltpu.VMEM((4, PACK - PART, HALF), jnp.bfloat16),
            pltpu.VMEM((SIDE, PART, HALF), jnp.bfloat16),
            pltpu.VMEM((3, PACK - PART, HALF), jnp.bfloat16),
            pltpu.VMEM((SIDE, PACK, HALF), jnp.bfloat16),
            pltpu.VMEM((PACK_INV, HALF), jnp.bfloat16),
            pltpu.SMEM((BLOCKS,), jnp.int32),
            dma((8,)), dma((4,)), dma((4,)), dma((3,)), dma((3,)), dma((4, 2)), dma((4, 2)), dma((4,)), dma((4,)),
            dma((4,)), dma((4,)), dma((3,)), dma((3,)),
            dma((4,)), dma((4,)), dma((4,)), dma((4,)), dma((4,)), dma((4,)), dma((4,)), dma((4,)), dma((8,)), dma((8,)),
            dma((3,)), dma((13,)), dma((13,)), dma((8,)), dma((8,)),
        ],
        compiler_params=pltpu.CompilerParams(
            collective_id=0, has_side_effects=True, vmem_limit_bytes=32 << 20
        ),
        cost_estimate=pl.CostEstimate(flops=5 * 10**9, bytes_accessed=32 << 20, transcendentals=0),
    )(activations, gradient.T, iterations)
    step = 8
    return pl.pallas_call(
        apply_kernel,
        name="apply",
        grid=(BLOCKS // step,),
        out_shape=jax.ShapeDtypeStruct((width, columns), jnp.bfloat16),
        in_specs=[
            pl.BlockSpec((step, PACK_INV, HALF), lambda i: (i, 0, 0)),
            pl.BlockSpec((columns, step * BS), lambda i: (0, i)),
        ],
        out_specs=pl.BlockSpec((step * BS, columns), lambda i: (i, 0)),
        compiler_params=pltpu.CompilerParams(vmem_limit_bytes=32 << 20),
        cost_estimate=pl.CostEstimate(flops=2 * 10**9, bytes_accessed=20 << 20, transcendentals=0),
    )(inverses.reshape(BLOCKS, PACK_INV, HALF), full)


def solution(mesh):
    placed = (P(("dp", "owner"), None), P(None, ("dp", "owner")), P())
    return jax.shard_map(
        per_device, mesh=mesh, in_specs=placed, out_specs=P(None, "dp"), check_vma=False
    )
```

```python
import functools

import jax
import jax.numpy as jnp
from jax import lax
from jax.experimental import pallas as pl
from jax.experimental.pallas import tpu as pltpu
from jax.sharding import PartitionSpec as P

BS = 256
HALF = BS // 2
BLOCKS = 32
PACK = BS + 16
PART = 144
PACK_INV = 2 * PART
TOKENS = 131072
DAMPING = 0.1
ITERS = 8
LEAST_ITERS = 5
SIDE = 4
GROUP = 4
GROUP_COLS = GROUP * BS
CLASS = 16
WRITE = 4
AHEAD = 4
AWAY = (2, 1, 3, 0)
X_EARLY = 4096
Y_EARLY = 2048
ACROSS = 2048
S2_FIRST = False
MESH = pl.DeviceIdType.MESH

TN = (((0,), (0,)), ((), ()))
NT = (((1,), (1,)), ((), ()))


def here():
    shard = lax.axis_index("dp")
    owner = lax.axis_index("owner")
    x = (owner // 8) * 2 + shard % 2
    return x, (owner // 2) % 4, shard // 2, owner % 2


def mesh_id(x, y, z, core):
    return (z * 2 + x % 2, (x // 2) * 8 + y * 2 + core)


def owner_of(x, y, core):
    return (x // 2) * 8 + y * 2 + core


def tile_iota():
    rows = lax.broadcasted_iota(jnp.int32, (HALF, HALF), 0)
    cols = lax.broadcasted_iota(jnp.int32, (HALF, HALF), 1)
    return rows, cols


def pack(block):
    rows, cols = tile_iota()
    low = block[HALF:, HALF:]
    mixed = jnp.where(rows <= cols, block[:HALF, :HALF], low)
    diagonal = jnp.sum(jnp.where(rows == cols, low, 0.0), axis=0, keepdims=True)
    return mixed, block[:HALF, HALF:], jnp.broadcast_to(diagonal, (16, HALF))


def unpack(mixed, off, diagonal):
    rows, cols = tile_iota()
    turned = mixed.T
    first = jnp.where(rows <= cols, mixed, turned)
    second = jnp.where(rows > cols, mixed, jnp.where(rows < cols, turned, diagonal))
    return first, off, off.T, second


def split(value):
    high = value.astype(jnp.bfloat16)
    return high, (value - high.astype(jnp.float32)).astype(jnp.bfloat16)


def dot3(left, right):
    lh, ll = split(left)
    rh, rl = split(right)
    mul = functools.partial(jnp.dot, preferred_element_type=jnp.float32)
    return mul(lh, rh) + (mul(lh, rl) + mul(ll, rh))


def newton(factor, count):
    rows = lax.broadcasted_iota(jnp.int32, (BS, BS), 0)
    cols = lax.broadcasted_iota(jnp.int32, (BS, BS), 1)
    identity = jnp.where(rows == cols, 1.0, 0.0)
    damped = factor / TOKENS + DAMPING * identity
    bound = jnp.max(jnp.sum(jnp.abs(damped), axis=1))
    ratio = damped / bound
    approx = (2.0 * identity - ratio) / bound
    ratio = 2.0 * ratio - dot3(ratio, ratio)
    for step in range(1, ITERS):
        if step < ITERS - 1:
            both = dot3(jnp.concatenate([ratio, approx], axis=0), ratio)
            later = 2.0 * approx - both[BS:]
            ratio = 2.0 * ratio - both[:BS]
        else:
            later = 2.0 * approx - dot3(approx, ratio)
        approx = later if step < LEAST_ITERS else jnp.where(step < count, later, approx)
    return approx


def factor_kernel(
    act_ref, grad_ref, iters_ref,
    full_ref, inv_ref,
    act, to_sib, from_sib, own, summed, z_land, x_land, x_terms, z_terms, x_last, z_last, y_terms, inv_own, count,
    act_sem, sib_send, sib_recv, z_send, z_recv, x_send, x_recv, y_send, y_recv, x2_send, x2_recv, z2_send, z2_recv,
    agx_send, agx_recv, agz_send, agz_recv, agx2_send, agx2_recv, agz2_send, agz2_recv, ags_send, ags_recv,
    local_sem, g_send, g_recv, gs_send, gs_recv,
):
    x, y, z, core = here()
    sibling = mesh_id(x, y, z, 1 - core)

    def at(dx, dy, dz):
        return mesh_id((x + dx) % SIDE, (y + dy) % SIDE, (z + dz) % SIDE, core)

    def remote(src, dst, send, recv, target):
        return pltpu.make_async_remote_copy(
            src_ref=src, dst_ref=dst, send_sem=send, recv_sem=recv, device_id=target, device_id_type=MESH
        )

    work = [("sib", 0), ("sib", 1), ("own", 0), ("sib", 2), ("own", 1), ("sib", 3), ("own", 2), ("own", 3)]

    def act_copy(slot):
        kind, k = work[slot]
        side = 1 - core if kind == "sib" else core
        group = side * 4 + (z + AWAY[k]) % SIDE
        cols = pl.ds(pl.multiple_of(group * GROUP_COLS, GROUP_COLS), GROUP_COLS)
        return pltpu.make_async_copy(act_ref.at[:, cols], act.at[slot], act_sem.at[slot])

    for slot in range(AHEAD):
        act_copy(slot).start()
    counts = pltpu.make_async_copy(iters_ref, count, local_sem.at[2])
    counts.start()

    barrier = pltpu.get_barrier_semaphore()
    partners = [sibling]
    for d in (1, 2, 3):
        partners += [at(0, d, 0), at(d, 0, 0), at(0, 0, d)]
    for partner in partners:
        pl.semaphore_signal(barrier, inc=1, device_id=partner, device_id_type=MESH)

    def products(slot, store):
        act_copy(slot).wait()
        if slot + AHEAD < 8:
            act_copy(slot + AHEAD).start()
        for j in range(GROUP):
            cols = act[slot, :, j * BS : (j + 1) * BS]
            mixed, off, diagonal = pack(lax.dot_general(cols, cols, TN, preferred_element_type=jnp.float32))
            store(j, 0, HALF, mixed)
            store(j, HALF, HALF, off)
            store(j, BS, 16, diagonal)

    def sib_products(slot):
        k = work[slot][1]

        def store(j, first, rows, value):
            to_sib[k, j, first : first + rows] = value.astype(jnp.bfloat16)

        products(slot, store)

    sib_products(0)
    pl.semaphore_wait(barrier, len(partners))

    def rows_of(dx, dy, first, rows, cols=slice(None)):
        start = owner_of((x + dx) % SIDE, (y + dy) % SIDE, core) * 32 + first
        return full_ref.at[pl.ds(pl.multiple_of(start, 16), rows), cols]

    def shard(dx, dy):
        return rows_of(dx, dy, 0, 32)

    mine = pltpu.make_async_copy(grad_ref, shard(0, 0), local_sem.at[0])
    mine.start()
    gathers = []

    def gather(index, dx, dy, place, src=None):
        copy = remote(place if src is None else src, place, g_send.at[index], g_recv.at[index], at(dx, dy, 0))
        copy.start()
        gathers.append(copy)

    def arrived(index, place):
        remote(place, place, g_send.at[index], g_recv.at[index], at(0, 1, 0)).wait_recv()

    passes = []

    def to_sibling(index, place, src=None):
        copy = remote(place if src is None else src, place, gs_send.at[index], gs_recv.at[index], sibling)
        copy.start()
        passes.append(copy)

    def columns(first, last):
        return pl.ds(first, last - first)

    def send_parts(index, dx, dy, first, last, src=None):
        cols = columns(first, last)
        gather(index, dx, dy, rows_of(0, 0, 0, 32, cols) if src is None else src, grad_ref.at[:, cols] if src is None else None)

    width = grad_ref.shape[1]
    gather(0, 0, 1, shard(0, 0), grad_ref)
    gather(1, 0, 3, shard(0, 0), grad_ref)
    send_parts(2, 2, 0, 0, X_EARLY)

    def sib_copy(k):
        return remote(to_sib.at[k], from_sib.at[k], sib_send.at[k], sib_recv.at[k], sibling)

    def z_copy(k):
        return remote(summed.at[k, :, :PART], z_land.at[k], z_send.at[k], z_recv.at[k], at(0, 0, AWAY[k]))

    def x_copy(dx, k):
        return remote(
            summed.at[k : k + 2, (x + dx) % SIDE, PART:], x_land.at[dx, k : k + 2],
            x_send.at[dx, k // 2], x_recv.at[dx, k // 2], at(dx, 0, 0),
        )

    sib_copy(0).start()
    for slot in range(1, 8):
        kind, k = work[slot]
        if kind == "sib":
            sib_products(slot)
            sib_copy(k).start()
            continue

        def store_own(j, first, rows, value):
            own[j, first : first + rows] = value

        products(slot, store_own)
        sib_copy(k).wait_recv()
        summed[k] = (own[...] + from_sib[k].astype(jnp.float32)).astype(jnp.bfloat16)
        if k < 3:
            z_copy(k).start()
        if k % 2:
            for dx in (2, 1, 3):
                x_copy(dx, k - 1).start()

    to_sibling(0, shard(0, 0), grad_ref)

    totals = own[:, :PART] + from_sib[3, :, :PART].astype(jnp.float32)
    for k in range(3):
        z_copy(k).wait_recv()
        totals = totals + z_land[k].astype(jnp.float32)
    x_terms[...] = totals.astype(jnp.bfloat16)

    def x_copy2(dx):
        return remote(x_terms.at[(x + dx) % SIDE], x_last.at[dx], x2_send.at[dx], x2_recv.at[dx], at(dx, 0, 0))

    def z_copy2(k):
        return remote(z_terms.at[k], z_last.at[k], z2_send.at[k], z2_recv.at[k], at(0, 0, AWAY[k]))

    for dx in (2, 1, 3):
        x_copy2(dx).start()
    for half in (0, 2):
        for dx in (1, 3, 2):
            x_copy(dx, half).wait_recv()
        for k in (half, half + 1):
            mine_here = summed[k, pl.ds(x, 1), PART:][0].astype(jnp.float32)
            for dx in (1, 3, 2):
                mine_here = mine_here + x_land[dx, k].astype(jnp.float32)
            z_terms[k] = mine_here.astype(jnp.bfloat16)
            if k < 3:
                z_copy2(k).start()

    if X_EARLY < width:
        send_parts(3, 2, 0, X_EARLY, width)
    arrived(2, rows_of(2, 0, 0, 32, columns(0, X_EARLY)))
    if Y_EARLY:
        send_parts(4, 0, 1, 0, Y_EARLY, rows_of(2, 0, 0, 32, columns(0, Y_EARLY)))
        send_parts(5, 0, 3, 0, Y_EARLY, rows_of(2, 0, 0, 32, columns(0, Y_EARLY)))

    first = x_terms[pl.ds(x, 1)][0].astype(jnp.float32)
    for dx in (1, 3, 2):
        x_copy2(dx).wait_recv()
        first = first + x_last[dx].astype(jnp.float32)
    rest = z_terms[3].astype(jnp.float32)
    for k in (1, 2, 0):
        z_copy2(k).wait_recv()
        rest = rest + z_last[k].astype(jnp.float32)
    y_terms[pl.ds(y, 1), :PART] = first.astype(jnp.bfloat16)[None]
    y_terms[pl.ds(y, 1), PART:] = rest.astype(jnp.bfloat16)[None]

    def y_copy(dy):
        return remote(y_terms.at[y], y_terms.at[y], y_send.at[dy], y_recv.at[dy], at(0, dy, 0))

    def send_opposite():
        arrived(6, rows_of(0, 2, 0, 16))
        arrived(7, rows_of(0, 2, 16, 16))
        if ACROSS:
            gather(10, 2, 0, rows_of(0, 2, 0, 32, columns(0, ACROSS)))
        to_sibling(4, shard(0, 2))

    for dy in (2, 1, 3):
        y_copy(dy).start()

    arrived(0, shard(0, 3))
    gather(6, 0, 1, rows_of(0, 3, 0, 16))
    arrived(1, shard(0, 1))
    gather(7, 0, 3, rows_of(0, 1, 16, 16))
    to_sibling(1, shard(0, 3))
    to_sibling(2, shard(0, 1))
    for dy in (1, 3, 2):
        y_copy(dy).wait_recv()

    if X_EARLY < width:
        arrived(3, rows_of(2, 0, 0, 32, columns(X_EARLY, width)))
    send_parts(8, 0, 1, Y_EARLY, width, rows_of(2, 0, 0, 32, columns(Y_EARLY, width)))
    send_parts(9, 0, 3, Y_EARLY, width, rows_of(2, 0, 0, 32, columns(Y_EARLY, width)))
    to_sibling(3, shard(2, 0))
    if S2_FIRST:
        send_opposite()

    terms = [y_terms[i].astype(jnp.float32) for i in range(SIDE)]
    whole = (terms[0] + terms[1]) + (terms[2] + terms[3])
    c00, c01, c10, c11 = unpack(whole[:HALF], whole[HALF:BS], whole[BS : BS + 1])
    factor = jnp.concatenate(
        [jnp.concatenate([c00, c01], axis=1), jnp.concatenate([c10, c11], axis=1)], axis=0
    )
    block = core * CLASS + z * 4 + x
    counts.wait()
    mixed, off, diagonal = pack(newton(factor, count[block]))
    inv_own[:HALF] = mixed.astype(jnp.bfloat16)
    inv_own[HALF:BS] = off.astype(jnp.bfloat16)
    inv_own[BS:PACK] = diagonal.astype(jnp.bfloat16)
    inv_own[PACK:] = jnp.zeros((PACK_INV - PACK, HALF), jnp.bfloat16)

    upper, lower = pl.ds(0, PART), pl.ds(PART, PART)

    def agx_copy(d):
        return remote(inv_own.at[upper], inv_ref.at[core, z, x, upper], agx_send.at[d], agx_recv.at[d], at(d, 0, 0))

    def agz_copy(d):
        return remote(inv_own.at[lower], inv_ref.at[core, z, x, lower], agz_send.at[d], agz_recv.at[d], at(0, 0, d))

    def along_x(d):
        return inv_ref.at[core, (z + SIDE - d) % SIDE, :, upper]

    def along_z(d):
        return inv_ref.at[core, :, (x + SIDE - d) % SIDE, lower]

    def agz_copy2(d):
        return remote(along_x(0), along_x(0), agz2_send.at[d], agz2_recv.at[d], at(0, 0, d))

    def agx_copy2(d):
        return remote(along_z(0), along_z(0), agx2_send.at[d], agx2_recv.at[d], at(d, 0, 0))

    def pass_on(place, slot):
        return remote(place, place, ags_send.at[slot], ags_recv.at[slot], sibling)

    for d in (2, 1, 3):
        agx_copy(d).start()
        agz_copy(d).start()
    keep = pltpu.make_async_copy(inv_own, inv_ref.at[core, z, x], local_sem.at[1])
    keep.start()
    keep.wait()
    for d in (1, 3, 2):
        agx_copy(d).wait_recv()
    for d in (2, 1, 3):
        agz_copy2(d).start()
    for d in (1, 3, 2):
        agz_copy(d).wait_recv()
    for d in (2, 1, 3):
        agx_copy2(d).start()
    pass_on(along_x(0), 0).start()
    pass_on(along_z(0), 4).start()
    if not S2_FIRST:
        send_opposite()
    for dy, one, two in ((3, 4, 8), (1, 5, 9)):
        if Y_EARLY:
            arrived(one, rows_of(2, dy, 0, 32, columns(0, Y_EARLY)))
        arrived(two, rows_of(2, dy, 0, 32, columns(Y_EARLY, width)))
        if ACROSS < width:
            first_row = 0 if dy == 3 else 16
            gather(11 + first_row // 16, 0, 4 - dy, rows_of(2, dy, first_row, 16, columns(ACROSS, width)))
        to_sibling(5 + first_row // 16 if ACROSS < width else 5 + dy // 2, shard(2, dy))
    for d in (1, 3, 2):
        agz_copy2(d).wait_recv()
        pass_on(along_x(d), d).start()
        agx_copy2(d).wait_recv()
        pass_on(along_z(d), 4 + d).start()
    if ACROSS:
        arrived(10, rows_of(2, 2, 0, 32, columns(0, ACROSS)))
    if ACROSS < width:
        arrived(11, rows_of(2, 2, 0, 16, columns(ACROSS, width)))
        arrived(12, rows_of(2, 2, 16, 16, columns(ACROSS, width)))
    to_sibling(7, shard(2, 2))

    mine.wait()
    for copy in gathers:
        copy.wait_send()
    for k in range(4):
        sib_copy(k).wait_send()
    for k in range(3):
        z_copy(k).wait_send()
        z_copy2(k).wait_send()
    for d in (1, 2, 3):
        x_copy(d, 0).wait_send()
        x_copy(d, 2).wait_send()
        x_copy2(d).wait_send()
        y_copy(d).wait_send()
        agx_copy(d).wait_send()
        agz_copy(d).wait_send()
        agx_copy2(d).wait_send()
        agz_copy2(d).wait_send()
    for d in range(4):
        pass_on(along_x(d), d).wait()
        pass_on(along_z(d), 4 + d).wait()
    for copy in passes:
        copy.wait()


def apply_kernel(inv_ref, grad_ref, out_ref, stage, sem):
    def block_copy(b):
        rows = pl.ds(b * BS, BS)
        return pltpu.make_async_copy(stage.at[rows], out_ref.at[rows], sem.at[b])

    for b in range(BLOCKS):
        packed = inv_ref[b].astype(jnp.float32)
        parts = unpack(packed[:HALF], packed[HALF:BS], packed[BS : BS + 1])
        c00, c01, c10, c11 = [part.astype(jnp.bfloat16) for part in parts]
        inverse = jnp.concatenate(
            [jnp.concatenate([c00, c01], axis=1), jnp.concatenate([c10, c11], axis=1)], axis=0
        )
        rows = grad_ref[:, b * BS : (b + 1) * BS]
        stage[b * BS : (b + 1) * BS] = lax.dot_general(
            inverse, rows, NT, preferred_element_type=jnp.float32
        ).astype(jnp.bfloat16)
        if b % WRITE == WRITE - 1:
            for w in range(b - WRITE + 1, b + 1):
                block_copy(w).start()
    for b in range(BLOCKS):
        block_copy(b).wait()


def per_device(activations, gradient, iterations):
    width = activations.shape[1]
    columns = gradient.shape[1] * 16
    anywhere = pl.BlockSpec(memory_space=pl.ANY)
    hbm = pl.BlockSpec(memory_space=pltpu.HBM)
    dma = pltpu.SemaphoreType.DMA
    full, inverses = pl.pallas_call(
        factor_kernel,
        name="factor",
        out_shape=[
            jax.ShapeDtypeStruct((columns, width), jnp.bfloat16),
            jax.ShapeDtypeStruct((2, SIDE, SIDE, PACK_INV, HALF), jnp.bfloat16),
        ],
        in_specs=[hbm, hbm, hbm],
        out_specs=[anywhere, anywhere],
        scratch_shapes=[
            pltpu.VMEM((8, activations.shape[0], GROUP_COLS), jnp.bfloat16),
            pltpu.VMEM((4, GROUP, PACK, HALF), jnp.bfloat16),
            pltpu.VMEM((4, GROUP, PACK, HALF), jnp.bfloat16),
            pltpu.VMEM((GROUP, PACK, HALF), jnp.float32),
            pltpu.VMEM((4, GROUP, PACK, HALF), jnp.bfloat16),
            pltpu.VMEM((3, GROUP, PART, HALF), jnp.bfloat16),
            pltpu.VMEM((SIDE, 4, PACK - PART, HALF), jnp.bfloat16),
            pltpu.VMEM((GROUP, PART, HALF), jnp.bfloat16),
            pltpu.VMEM((4, PACK - PART, HALF), jnp.bfloat16),
            pltpu.VMEM((SIDE, PART, HALF), jnp.bfloat16),
            pltpu.VMEM((3, PACK - PART, HALF), jnp.bfloat16),
            pltpu.VMEM((SIDE, PACK, HALF), jnp.bfloat16),
            pltpu.VMEM((PACK_INV, HALF), jnp.bfloat16),
            pltpu.SMEM((BLOCKS,), jnp.int32),
            dma((8,)), dma((4,)), dma((4,)), dma((3,)), dma((3,)), dma((4, 2)), dma((4, 2)), dma((4,)), dma((4,)),
            dma((4,)), dma((4,)), dma((3,)), dma((3,)),
            dma((4,)), dma((4,)), dma((4,)), dma((4,)), dma((4,)), dma((4,)), dma((4,)), dma((4,)), dma((8,)), dma((8,)),
            dma((3,)), dma((13,)), dma((13,)), dma((8,)), dma((8,)),
        ],
        compiler_params=pltpu.CompilerParams(
            collective_id=0, has_side_effects=True, vmem_limit_bytes=32 << 20
        ),
        cost_estimate=pl.CostEstimate(flops=5 * 10**9, bytes_accessed=32 << 20, transcendentals=0),
    )(activations, pltpu.with_memory_space_constraint(gradient.T, pltpu.HBM), pltpu.with_memory_space_constraint(iterations, pltpu.HBM))
    vmem = pl.BlockSpec(memory_space=pltpu.VMEM)
    return pl.pallas_call(
        apply_kernel,
        name="apply",
        out_shape=jax.ShapeDtypeStruct((width, columns), jnp.bfloat16),
        in_specs=[vmem, vmem],
        out_specs=pl.BlockSpec(memory_space=pltpu.HBM),
        scratch_shapes=[pltpu.VMEM((width, columns), jnp.bfloat16), dma((BLOCKS,))],
        compiler_params=pltpu.CompilerParams(vmem_limit_bytes=32 << 20),
        cost_estimate=pl.CostEstimate(flops=2 * 10**9, bytes_accessed=20 << 20, transcendentals=0),
    )(inverses.reshape(BLOCKS, PACK_INV, HALF), full)


def solution(mesh):
    placed = (P(("dp", "owner"), None), P(None, ("dp", "owner")), P())
    return jax.shard_map(
        per_device, mesh=mesh, in_specs=placed, out_specs=P(None, "dp"), check_vma=False
    )
```

```python
import functools

import jax
import jax.numpy as jnp
from jax import lax
from jax.experimental import pallas as pl
from jax.experimental.pallas import tpu as pltpu
from jax.sharding import PartitionSpec as P

BS = 256
HALF = BS // 2
BLOCKS = 32
PACK = BS + 16
PART = 144
PACK_INV = 2 * PART
TOKENS = 131072
DAMPING = 0.1
ITERS = 8
LEAST_ITERS = 5
SIDE = 4
GROUP = 4
GROUP_COLS = GROUP * BS
CLASS = 16
WRITE = 4
AHEAD = 4
AWAY = (2, 1, 3, 0)
X_EARLY = 3072
Y_EARLY = 2048
ACROSS = 2048
MESH = pl.DeviceIdType.MESH

TN = (((0,), (0,)), ((), ()))
NT = (((1,), (1,)), ((), ()))


def here():
    shard = lax.axis_index("dp")
    owner = lax.axis_index("owner")
    x = (owner // 8) * 2 + shard % 2
    return x, (owner // 2) % 4, shard // 2, owner % 2


def mesh_id(x, y, z, core):
    return (z * 2 + x % 2, (x // 2) * 8 + y * 2 + core)


def owner_of(x, y, core):
    return (x // 2) * 8 + y * 2 + core


def tile_iota():
    rows = lax.broadcasted_iota(jnp.int32, (HALF, HALF), 0)
    cols = lax.broadcasted_iota(jnp.int32, (HALF, HALF), 1)
    return rows, cols


def pack(block):
    rows, cols = tile_iota()
    low = block[HALF:, HALF:]
    mixed = jnp.where(rows <= cols, block[:HALF, :HALF], low)
    diagonal = jnp.sum(jnp.where(rows == cols, low, 0.0), axis=0, keepdims=True)
    return mixed, block[:HALF, HALF:], jnp.broadcast_to(diagonal, (16, HALF))


def unpack(mixed, off, diagonal):
    rows, cols = tile_iota()
    turned = mixed.T
    first = jnp.where(rows <= cols, mixed, turned)
    second = jnp.where(rows > cols, mixed, jnp.where(rows < cols, turned, diagonal))
    return first, off, off.T, second


def split(value):
    high = value.astype(jnp.bfloat16)
    return high, (value - high.astype(jnp.float32)).astype(jnp.bfloat16)


def dot3(left, right):
    lh, ll = split(left)
    rh, rl = split(right)
    mul = functools.partial(jnp.dot, preferred_element_type=jnp.float32)
    return mul(lh, rh) + (mul(lh, rl) + mul(ll, rh))


def newton(factor, count):
    rows = lax.broadcasted_iota(jnp.int32, (BS, BS), 0)
    cols = lax.broadcasted_iota(jnp.int32, (BS, BS), 1)
    identity = jnp.where(rows == cols, 1.0, 0.0)
    damped = factor / TOKENS + DAMPING * identity
    bound = jnp.max(jnp.sum(jnp.abs(damped), axis=1))
    ratio = damped / bound
    approx = (2.0 * identity - ratio) / bound
    ratio = 2.0 * ratio - dot3(ratio, ratio)
    for step in range(1, ITERS):
        if step < ITERS - 1:
            both = dot3(jnp.concatenate([ratio, approx], axis=0), ratio)
            later = 2.0 * approx - both[BS:]
            ratio = 2.0 * ratio - both[:BS]
        else:
            later = 2.0 * approx - dot3(approx, ratio)
        approx = later if step < LEAST_ITERS else jnp.where(step < count, later, approx)
    return approx


def factor_kernel(
    act_ref, grad_ref, iters_ref,
    full_ref, inv_ref,
    act, to_sib, from_sib, own, summed, z_land, x_land, x_terms, z_terms, x_last, z_last, y_terms, inv_own, count,
    act_sem, sib_send, sib_recv, z_send, z_recv, x_send, x_recv, y_send, y_recv, x2_send, x2_recv, z2_send, z2_recv,
    agx_send, agx_recv, agz_send, agz_recv, agx2_send, agx2_recv, agz2_send, agz2_recv, ags_send, ags_recv,
    local_sem, g_send, g_recv, gs_send, gs_recv,
):
    x, y, z, core = here()
    sibling = mesh_id(x, y, z, 1 - core)

    def at(dx, dy, dz):
        return mesh_id((x + dx) % SIDE, (y + dy) % SIDE, (z + dz) % SIDE, core)

    def remote(src, dst, send, recv, target):
        return pltpu.make_async_remote_copy(
            src_ref=src, dst_ref=dst, send_sem=send, recv_sem=recv, device_id=target, device_id_type=MESH
        )

    work = [("sib", 0), ("sib", 1), ("own", 0), ("sib", 2), ("own", 1), ("sib", 3), ("own", 2), ("own", 3)]

    def act_copy(slot):
        kind, k = work[slot]
        side = 1 - core if kind == "sib" else core
        group = side * 4 + (z + AWAY[k]) % SIDE
        cols = pl.ds(pl.multiple_of(group * GROUP_COLS, GROUP_COLS), GROUP_COLS)
        return pltpu.make_async_copy(act_ref.at[:, cols], act.at[slot], act_sem.at[slot])

    for slot in range(AHEAD):
        act_copy(slot).start()
    counts = pltpu.make_async_copy(iters_ref, count, local_sem.at[2])
    counts.start()

    barrier = pltpu.get_barrier_semaphore()
    partners = [sibling]
    for d in (1, 2, 3):
        partners += [at(0, d, 0), at(d, 0, 0), at(0, 0, d)]
    for partner in partners:
        pl.semaphore_signal(barrier, inc=1, device_id=partner, device_id_type=MESH)

    def products(slot, store):
        act_copy(slot).wait()
        if slot + AHEAD < 8:
            act_copy(slot + AHEAD).start()
        for j in range(GROUP):
            cols = act[slot, :, j * BS : (j + 1) * BS]
            mixed, off, diagonal = pack(lax.dot_general(cols, cols, TN, preferred_element_type=jnp.float32))
            store(j, 0, HALF, mixed)
            store(j, HALF, HALF, off)
            store(j, BS, 16, diagonal)

    def sib_products(slot):
        k = work[slot][1]

        def store(j, first, rows, value):
            to_sib[k, j, first : first + rows] = value.astype(jnp.bfloat16)

        products(slot, store)

    sib_products(0)
    pl.semaphore_wait(barrier, len(partners))

    def rows_of(dx, dy, first, rows, cols=slice(None)):
        start = owner_of((x + dx) % SIDE, (y + dy) % SIDE, core) * 32 + first
        return full_ref.at[pl.ds(pl.multiple_of(start, 16), rows), cols]

    def shard(dx, dy):
        return rows_of(dx, dy, 0, 32)

    mine = pltpu.make_async_copy(grad_ref, shard(0, 0), local_sem.at[0])
    mine.start()
    gathers = []

    def gather(index, dx, dy, place, src=None):
        copy = remote(place if src is None else src, place, g_send.at[index], g_recv.at[index], at(dx, dy, 0))
        copy.start()
        gathers.append(copy)

    def arrived(index, place):
        remote(place, place, g_send.at[index], g_recv.at[index], at(0, 1, 0)).wait_recv()

    passes = []

    def to_sibling(index, place, src=None):
        copy = remote(place if src is None else src, place, gs_send.at[index], gs_recv.at[index], sibling)
        copy.start()
        passes.append(copy)

    def columns(first, last):
        return pl.ds(first, last - first)

    def send_parts(index, dx, dy, first, last, src=None):
        cols = columns(first, last)
        gather(index, dx, dy, rows_of(0, 0, 0, 32, cols) if src is None else src, grad_ref.at[:, cols] if src is None else None)

    width = grad_ref.shape[1]
    gather(0, 0, 1, shard(0, 0), grad_ref)
    gather(1, 0, 3, shard(0, 0), grad_ref)
    send_parts(2, 2, 0, 0, X_EARLY)

    def sib_copy(k):
        return remote(to_sib.at[k], from_sib.at[k], sib_send.at[k], sib_recv.at[k], sibling)

    def z_copy(k):
        return remote(summed.at[k, :, :PART], z_land.at[k], z_send.at[k], z_recv.at[k], at(0, 0, AWAY[k]))

    def x_copy(dx, k):
        return remote(
            summed.at[k : k + 2, (x + dx) % SIDE, PART:], x_land.at[dx, k : k + 2],
            x_send.at[dx, k // 2], x_recv.at[dx, k // 2], at(dx, 0, 0),
        )

    sib_copy(0).start()
    for slot in range(1, 8):
        kind, k = work[slot]
        if kind == "sib":
            sib_products(slot)
            sib_copy(k).start()
            continue

        def store_own(j, first, rows, value):
            own[j, first : first + rows] = value

        products(slot, store_own)
        sib_copy(k).wait_recv()
        summed[k] = (own[...] + from_sib[k].astype(jnp.float32)).astype(jnp.bfloat16)
        if k < 3:
            z_copy(k).start()
        if k % 2:
            for dx in (2, 1, 3):
                x_copy(dx, k - 1).start()

    to_sibling(0, shard(0, 0), grad_ref)

    totals = own[:, :PART] + from_sib[3, :, :PART].astype(jnp.float32)
    for k in range(3):
        z_copy(k).wait_recv()
        totals = totals + z_land[k].astype(jnp.float32)
    x_terms[...] = totals.astype(jnp.bfloat16)

    def x_copy2(dx):
        return remote(x_terms.at[(x + dx) % SIDE], x_last.at[dx], x2_send.at[dx], x2_recv.at[dx], at(dx, 0, 0))

    def z_copy2(k):
        return remote(z_terms.at[k], z_last.at[k], z2_send.at[k], z2_recv.at[k], at(0, 0, AWAY[k]))

    for dx in (2, 1, 3):
        x_copy2(dx).start()
    for half in (0, 2):
        for dx in (1, 3, 2):
            x_copy(dx, half).wait_recv()
        for k in (half, half + 1):
            mine_here = summed[k, pl.ds(x, 1), PART:][0].astype(jnp.float32)
            for dx in (1, 3, 2):
                mine_here = mine_here + x_land[dx, k].astype(jnp.float32)
            z_terms[k] = mine_here.astype(jnp.bfloat16)
            if k < 3:
                z_copy2(k).start()

    arrived(2, rows_of(2, 0, 0, 32, columns(0, X_EARLY)))
    if Y_EARLY:
        send_parts(4, 0, 1, 0, Y_EARLY, rows_of(2, 0, 0, 32, columns(0, Y_EARLY)))
        send_parts(5, 0, 3, 0, Y_EARLY, rows_of(2, 0, 0, 32, columns(0, Y_EARLY)))

    first = x_terms[pl.ds(x, 1)][0].astype(jnp.float32)
    for dx in (1, 3, 2):
        x_copy2(dx).wait_recv()
        first = first + x_last[dx].astype(jnp.float32)
    rest = z_terms[3].astype(jnp.float32)
    for k in (1, 2, 0):
        z_copy2(k).wait_recv()
        rest = rest + z_last[k].astype(jnp.float32)
    y_terms[pl.ds(y, 1), :PART] = first.astype(jnp.bfloat16)[None]
    y_terms[pl.ds(y, 1), PART:] = rest.astype(jnp.bfloat16)[None]

    def y_copy(dy):
        return remote(y_terms.at[y], y_terms.at[y], y_send.at[dy], y_recv.at[dy], at(0, dy, 0))

    def send_opposite():
        arrived(6, rows_of(0, 2, 0, 16))
        arrived(7, rows_of(0, 2, 16, 16))
        if ACROSS:
            gather(10, 2, 0, rows_of(0, 2, 0, 32, columns(0, ACROSS)))
        to_sibling(4, shard(0, 2))

    for dy in (2, 1, 3):
        y_copy(dy).start()

    if X_EARLY < width:
        send_parts(3, 2, 0, X_EARLY, width)
    arrived(0, shard(0, 3))
    gather(6, 0, 1, rows_of(0, 3, 0, 16))
    arrived(1, shard(0, 1))
    gather(7, 0, 3, rows_of(0, 1, 16, 16))
    to_sibling(1, shard(0, 3))
    to_sibling(2, shard(0, 1))
    for dy in (1, 3, 2):
        y_copy(dy).wait_recv()

    terms = [y_terms[i].astype(jnp.float32) for i in range(SIDE)]
    whole = (terms[0] + terms[1]) + (terms[2] + terms[3])
    c00, c01, c10, c11 = unpack(whole[:HALF], whole[HALF:BS], whole[BS : BS + 1])
    factor = jnp.concatenate(
        [jnp.concatenate([c00, c01], axis=1), jnp.concatenate([c10, c11], axis=1)], axis=0
    )
    block = core * CLASS + z * 4 + x
    counts.wait()
    mixed, off, diagonal = pack(newton(factor, count[block]))
    inv_own[:HALF] = mixed.astype(jnp.bfloat16)
    inv_own[HALF:BS] = off.astype(jnp.bfloat16)
    inv_own[BS:PACK] = diagonal.astype(jnp.bfloat16)
    inv_own[PACK:] = jnp.zeros((PACK_INV - PACK, HALF), jnp.bfloat16)

    upper, lower = pl.ds(0, PART), pl.ds(PART, PART)

    def agx_copy(d):
        return remote(inv_own.at[upper], inv_ref.at[core, z, x, upper], agx_send.at[d], agx_recv.at[d], at(d, 0, 0))

    def agz_copy(d):
        return remote(inv_own.at[lower], inv_ref.at[core, z, x, lower], agz_send.at[d], agz_recv.at[d], at(0, 0, d))

    def along_x(d):
        return inv_ref.at[core, (z + SIDE - d) % SIDE, :, upper]

    def along_z(d):
        return inv_ref.at[core, :, (x + SIDE - d) % SIDE, lower]

    def agz_copy2(d):
        return remote(along_x(0), along_x(0), agz2_send.at[d], agz2_recv.at[d], at(0, 0, d))

    def agx_copy2(d):
        return remote(along_z(0), along_z(0), agx2_send.at[d], agx2_recv.at[d], at(d, 0, 0))

    def pass_on(place, slot):
        return remote(place, place, ags_send.at[slot], ags_recv.at[slot], sibling)

    for d in (2, 1, 3):
        agx_copy(d).start()
        agz_copy(d).start()
    keep = pltpu.make_async_copy(inv_own, inv_ref.at[core, z, x], local_sem.at[1])
    keep.start()

    if X_EARLY < width:
        arrived(3, rows_of(2, 0, 0, 32, columns(X_EARLY, width)))
    send_parts(8, 0, 1, Y_EARLY, width, rows_of(2, 0, 0, 32, columns(Y_EARLY, width)))
    send_parts(9, 0, 3, Y_EARLY, width, rows_of(2, 0, 0, 32, columns(Y_EARLY, width)))
    to_sibling(3, shard(2, 0))
    keep.wait()
    for d in (1, 3, 2):
        agx_copy(d).wait_recv()
    for d in (2, 1, 3):
        agz_copy2(d).start()
    for d in (1, 3, 2):
        agz_copy(d).wait_recv()
    for d in (2, 1, 3):
        agx_copy2(d).start()
    pass_on(along_x(0), 0).start()
    pass_on(along_z(0), 4).start()
    send_opposite()
    for dy, one, two in ((3, 4, 8), (1, 5, 9)):
        if Y_EARLY:
            arrived(one, rows_of(2, dy, 0, 32, columns(0, Y_EARLY)))
        arrived(two, rows_of(2, dy, 0, 32, columns(Y_EARLY, width)))
        if ACROSS < width:
            first_row = 0 if dy == 3 else 16
            gather(11 + first_row // 16, 0, 4 - dy, rows_of(2, dy, first_row, 16, columns(ACROSS, width)))
        to_sibling(5 + first_row // 16 if ACROSS < width else 5 + dy // 2, shard(2, dy))
    for d in (1, 3, 2):
        agz_copy2(d).wait_recv()
        pass_on(along_x(d), d).start()
        agx_copy2(d).wait_recv()
        pass_on(along_z(d), 4 + d).start()
    if ACROSS:
        arrived(10, rows_of(2, 2, 0, 32, columns(0, ACROSS)))
    if ACROSS < width:
        arrived(11, rows_of(2, 2, 0, 16, columns(ACROSS, width)))
        arrived(12, rows_of(2, 2, 16, 16, columns(ACROSS, width)))
    to_sibling(7, shard(2, 2))

    mine.wait()
    for copy in gathers:
        copy.wait_send()
    for k in range(4):
        sib_copy(k).wait_send()
    for k in range(3):
        z_copy(k).wait_send()
        z_copy2(k).wait_send()
    for d in (1, 2, 3):
        x_copy(d, 0).wait_send()
        x_copy(d, 2).wait_send()
        x_copy2(d).wait_send()
        y_copy(d).wait_send()
        agx_copy(d).wait_send()
        agz_copy(d).wait_send()
        agx_copy2(d).wait_send()
        agz_copy2(d).wait_send()
    for d in range(4):
        pass_on(along_x(d), d).wait()
        pass_on(along_z(d), 4 + d).wait()
    for copy in passes:
        copy.wait()


def apply_kernel(inv_ref, grad_ref, out_ref, stage, sem):
    def block_copy(b):
        rows = pl.ds(b * BS, BS)
        return pltpu.make_async_copy(stage.at[rows], out_ref.at[rows], sem.at[b])

    for b in range(BLOCKS):
        packed = inv_ref[b].astype(jnp.float32)
        parts = unpack(packed[:HALF], packed[HALF:BS], packed[BS : BS + 1])
        c00, c01, c10, c11 = [part.astype(jnp.bfloat16) for part in parts]
        inverse = jnp.concatenate(
            [jnp.concatenate([c00, c01], axis=1), jnp.concatenate([c10, c11], axis=1)], axis=0
        )
        rows = grad_ref[:, b * BS : (b + 1) * BS]
        stage[b * BS : (b + 1) * BS] = lax.dot_general(
            inverse, rows, NT, preferred_element_type=jnp.float32
        ).astype(jnp.bfloat16)
        if b % WRITE == WRITE - 1:
            for w in range(b - WRITE + 1, b + 1):
                block_copy(w).start()
    for b in range(BLOCKS):
        block_copy(b).wait()


def per_device(activations, gradient, iterations):
    width = activations.shape[1]
    columns = gradient.shape[1] * 16
    anywhere = pl.BlockSpec(memory_space=pl.ANY)
    hbm = pl.BlockSpec(memory_space=pltpu.HBM)
    dma = pltpu.SemaphoreType.DMA
    full, inverses = pl.pallas_call(
        factor_kernel,
        name="factor",
        out_shape=[
            jax.ShapeDtypeStruct((columns, width), jnp.bfloat16),
            jax.ShapeDtypeStruct((2, SIDE, SIDE, PACK_INV, HALF), jnp.bfloat16),
        ],
        in_specs=[hbm, hbm, hbm],
        out_specs=[anywhere, anywhere],
        scratch_shapes=[
            pltpu.VMEM((8, activations.shape[0], GROUP_COLS), jnp.bfloat16),
            pltpu.VMEM((4, GROUP, PACK, HALF), jnp.bfloat16),
            pltpu.VMEM((4, GROUP, PACK, HALF), jnp.bfloat16),
            pltpu.VMEM((GROUP, PACK, HALF), jnp.float32),
            pltpu.VMEM((4, GROUP, PACK, HALF), jnp.bfloat16),
            pltpu.VMEM((3, GROUP, PART, HALF), jnp.bfloat16),
            pltpu.VMEM((SIDE, 4, PACK - PART, HALF), jnp.bfloat16),
            pltpu.VMEM((GROUP, PART, HALF), jnp.bfloat16),
            pltpu.VMEM((4, PACK - PART, HALF), jnp.bfloat16),
            pltpu.VMEM((SIDE, PART, HALF), jnp.bfloat16),
            pltpu.VMEM((3, PACK - PART, HALF), jnp.bfloat16),
            pltpu.VMEM((SIDE, PACK, HALF), jnp.bfloat16),
            pltpu.VMEM((PACK_INV, HALF), jnp.bfloat16),
            pltpu.SMEM((BLOCKS,), jnp.int32),
            dma((8,)), dma((4,)), dma((4,)), dma((3,)), dma((3,)), dma((4, 2)), dma((4, 2)), dma((4,)), dma((4,)),
            dma((4,)), dma((4,)), dma((3,)), dma((3,)),
            dma((4,)), dma((4,)), dma((4,)), dma((4,)), dma((4,)), dma((4,)), dma((4,)), dma((4,)), dma((8,)), dma((8,)),
            dma((3,)), dma((13,)), dma((13,)), dma((8,)), dma((8,)),
        ],
        compiler_params=pltpu.CompilerParams(
            collective_id=0, has_side_effects=True, vmem_limit_bytes=32 << 20
        ),
        cost_estimate=pl.CostEstimate(flops=5 * 10**9, bytes_accessed=32 << 20, transcendentals=0),
    )(activations, pltpu.with_memory_space_constraint(gradient.T, pltpu.HBM), pltpu.with_memory_space_constraint(iterations, pltpu.HBM))
    vmem = pl.BlockSpec(memory_space=pltpu.VMEM)
    return pl.pallas_call(
        apply_kernel,
        name="apply",
        out_shape=jax.ShapeDtypeStruct((width, columns), jnp.bfloat16),
        in_specs=[vmem, vmem],
        out_specs=pl.BlockSpec(memory_space=pltpu.HBM),
        scratch_shapes=[pltpu.VMEM((width, columns), jnp.bfloat16), dma((BLOCKS,))],
        compiler_params=pltpu.CompilerParams(vmem_limit_bytes=32 << 20),
        cost_estimate=pl.CostEstimate(flops=2 * 10**9, bytes_accessed=20 << 20, transcendentals=0),
    )(inverses.reshape(BLOCKS, PACK_INV, HALF), full)


def solution(mesh):
    placed = (P(("dp", "owner"), None), P(None, ("dp", "owner")), P())
    return jax.shard_map(
        per_device, mesh=mesh, in_specs=placed, out_specs=P(None, "dp"), check_vma=False
    )
```

```python
import functools

import jax
import jax.numpy as jnp
from jax import lax
from jax.experimental import pallas as pl
from jax.experimental.pallas import tpu as pltpu
from jax.sharding import PartitionSpec as P

BS = 256
HALF = BS // 2
BLOCKS = 32
PACK = BS + 16
PART = 144
PACK_INV = 2 * PART
TOKENS = 131072
DAMPING = 0.1
ITERS = 8
LEAST_ITERS = 5
SIDE = 4
GROUP = 4
GROUP_COLS = GROUP * BS
CLASS = 16
WRITE = 1
AHEAD = 4
AWAY = (2, 1, 3, 0)
X_EARLY = 2048
MIDDLE = 4096
Y_EARLY = 2048
ACROSS = 2048
MESH = pl.DeviceIdType.MESH

TN = (((0,), (0,)), ((), ()))
NT = (((1,), (1,)), ((), ()))


def here():
    shard = lax.axis_index("dp")
    owner = lax.axis_index("owner")
    x = (owner // 8) * 2 + shard % 2
    return x, (owner // 2) % 4, shard // 2, owner % 2


def mesh_id(x, y, z, core):
    return (z * 2 + x % 2, (x // 2) * 8 + y * 2 + core)


def owner_of(x, y, core):
    return (x // 2) * 8 + y * 2 + core


def tile_iota():
    rows = lax.broadcasted_iota(jnp.int32, (HALF, HALF), 0)
    cols = lax.broadcasted_iota(jnp.int32, (HALF, HALF), 1)
    return rows, cols


def pack(block):
    rows, cols = tile_iota()
    low = block[HALF:, HALF:]
    mixed = jnp.where(rows <= cols, block[:HALF, :HALF], low)
    diagonal = jnp.sum(jnp.where(rows == cols, low, 0.0), axis=0, keepdims=True)
    return mixed, block[:HALF, HALF:], jnp.broadcast_to(diagonal, (16, HALF))


def unpack(mixed, off, diagonal):
    rows, cols = tile_iota()
    turned = mixed.T
    first = jnp.where(rows <= cols, mixed, turned)
    second = jnp.where(rows > cols, mixed, jnp.where(rows < cols, turned, diagonal))
    return first, off, off.T, second


def split(value):
    high = value.astype(jnp.bfloat16)
    return high, (value - high.astype(jnp.float32)).astype(jnp.bfloat16)


def dot3(left, right):
    lh, ll = split(left)
    rh, rl = split(right)
    mul = functools.partial(jnp.dot, preferred_element_type=jnp.float32)
    return mul(lh, rh) + (mul(lh, rl) + mul(ll, rh))


def newton(factor, count):
    rows = lax.broadcasted_iota(jnp.int32, (BS, BS), 0)
    cols = lax.broadcasted_iota(jnp.int32, (BS, BS), 1)
    identity = jnp.where(rows == cols, 1.0, 0.0)
    damped = factor / TOKENS + DAMPING * identity
    bound = jnp.max(jnp.sum(jnp.abs(damped), axis=1))
    ratio = damped / bound
    approx = (2.0 * identity - ratio) / bound
    ratio = 2.0 * ratio - dot3(ratio, ratio)
    for step in range(1, ITERS):
        if step < ITERS - 1:
            both = dot3(jnp.concatenate([ratio, approx], axis=0), ratio)
            later = 2.0 * approx - both[BS:]
            ratio = 2.0 * ratio - both[:BS]
        else:
            later = 2.0 * approx - dot3(approx, ratio)
        approx = later if step < LEAST_ITERS else jnp.where(step < count, later, approx)
    return approx


def factor_kernel(
    act_ref, grad_ref, iters_ref,
    full_ref, inv_ref,
    act, to_sib, from_sib, own, summed, z_land, x_land, x_terms, z_terms, x_last, z_last, y_terms, inv_own, count,
    act_sem, sib_send, sib_recv, z_send, z_recv, x_send, x_recv, y_send, y_recv, x2_send, x2_recv, z2_send, z2_recv,
    agx_send, agx_recv, agz_send, agz_recv, agx2_send, agx2_recv, agz2_send, agz2_recv, ags_send, ags_recv,
    local_sem, g_send, g_recv, gs_send, gs_recv,
):
    x, y, z, core = here()
    sibling = mesh_id(x, y, z, 1 - core)

    def at(dx, dy, dz):
        return mesh_id((x + dx) % SIDE, (y + dy) % SIDE, (z + dz) % SIDE, core)

    def remote(src, dst, send, recv, target):
        return pltpu.make_async_remote_copy(
            src_ref=src, dst_ref=dst, send_sem=send, recv_sem=recv, device_id=target, device_id_type=MESH
        )

    work = [("sib", 0), ("sib", 1), ("own", 0), ("sib", 2), ("own", 1), ("sib", 3), ("own", 2), ("own", 3)]

    def act_copy(slot):
        kind, k = work[slot]
        side = 1 - core if kind == "sib" else core
        group = side * 4 + (z + AWAY[k]) % SIDE
        cols = pl.ds(pl.multiple_of(group * GROUP_COLS, GROUP_COLS), GROUP_COLS)
        return pltpu.make_async_copy(act_ref.at[:, cols], act.at[slot], act_sem.at[slot])

    for slot in range(AHEAD):
        act_copy(slot).start()
    counts = pltpu.make_async_copy(iters_ref, count, local_sem.at[2])
    counts.start()

    barrier = pltpu.get_barrier_semaphore()
    partners = [sibling]
    for d in (1, 2, 3):
        partners += [at(0, d, 0), at(d, 0, 0), at(0, 0, d)]
    for partner in partners:
        pl.semaphore_signal(barrier, inc=1, device_id=partner, device_id_type=MESH)

    def products(slot, store):
        act_copy(slot).wait()
        if slot + AHEAD < 8:
            act_copy(slot + AHEAD).start()
        for j in range(GROUP):
            cols = act[slot, :, j * BS : (j + 1) * BS]
            mixed, off, diagonal = pack(lax.dot_general(cols, cols, TN, preferred_element_type=jnp.float32))
            store(j, 0, HALF, mixed)
            store(j, HALF, HALF, off)
            store(j, BS, 16, diagonal)

    def sib_products(slot):
        k = work[slot][1]

        def store(j, first, rows, value):
            to_sib[k, j, first : first + rows] = value.astype(jnp.bfloat16)

        products(slot, store)

    sib_products(0)
    pl.semaphore_wait(barrier, len(partners))

    def rows_of(dx, dy, first, rows, cols=slice(None)):
        start = owner_of((x + dx) % SIDE, (y + dy) % SIDE, core) * 32 + first
        return full_ref.at[pl.ds(pl.multiple_of(start, 16), rows), cols]

    def shard(dx, dy):
        return rows_of(dx, dy, 0, 32)

    mine = pltpu.make_async_copy(grad_ref, shard(0, 0), local_sem.at[0])
    mine.start()
    gathers = []

    def gather(index, dx, dy, place, src=None):
        copy = remote(place if src is None else src, place, g_send.at[index], g_recv.at[index], at(dx, dy, 0))
        copy.start()
        gathers.append(copy)

    def arrived(index, place):
        remote(place, place, g_send.at[index], g_recv.at[index], at(0, 1, 0)).wait_recv()

    passes = []

    def to_sibling(index, place, src=None):
        copy = remote(place if src is None else src, place, gs_send.at[index], gs_recv.at[index], sibling)
        copy.start()
        passes.append(copy)

    def columns(first, last):
        return pl.ds(first, last - first)

    def send_parts(index, dx, dy, first, last, src=None):
        cols = columns(first, last)
        gather(index, dx, dy, rows_of(0, 0, 0, 32, cols) if src is None else src, grad_ref.at[:, cols] if src is None else None)

    width = grad_ref.shape[1]
    gather(0, 0, 1, shard(0, 0), grad_ref)
    gather(1, 0, 3, shard(0, 0), grad_ref)
    send_parts(2, 2, 0, 0, X_EARLY)

    def sib_copy(k):
        return remote(to_sib.at[k], from_sib.at[k], sib_send.at[k], sib_recv.at[k], sibling)

    def z_copy(k):
        return remote(summed.at[k, :, :PART], z_land.at[k], z_send.at[k], z_recv.at[k], at(0, 0, AWAY[k]))

    def x_copy(dx, k):
        return remote(
            summed.at[k : k + 2, (x + dx) % SIDE, PART:], x_land.at[dx, k : k + 2],
            x_send.at[dx, k // 2], x_recv.at[dx, k // 2], at(dx, 0, 0),
        )

    sib_copy(0).start()
    for slot in range(1, 8):
        kind, k = work[slot]
        if kind == "sib":
            sib_products(slot)
            sib_copy(k).start()
            continue

        def store_own(j, first, rows, value):
            own[j, first : first + rows] = value

        products(slot, store_own)
        sib_copy(k).wait_recv()
        summed[k] = (own[...] + from_sib[k].astype(jnp.float32)).astype(jnp.bfloat16)
        if k < 3:
            z_copy(k).start()
        if k % 2:
            for dx in (2, 1, 3):
                x_copy(dx, k - 1).start()

    to_sibling(0, shard(0, 0), grad_ref)

    totals = own[:, :PART] + from_sib[3, :, :PART].astype(jnp.float32)
    for k in range(3):
        z_copy(k).wait_recv()
        totals = totals + z_land[k].astype(jnp.float32)
    x_terms[...] = totals.astype(jnp.bfloat16)

    def x_copy2(dx):
        return remote(x_terms.at[(x + dx) % SIDE], x_last.at[dx], x2_send.at[dx], x2_recv.at[dx], at(dx, 0, 0))

    def z_copy2(k):
        return remote(z_terms.at[k], z_last.at[k], z2_send.at[k], z2_recv.at[k], at(0, 0, AWAY[k]))

    for dx in (2, 1, 3):
        x_copy2(dx).start()
    for half in (0, 2):
        for dx in (1, 3, 2):
            x_copy(dx, half).wait_recv()
        for k in (half, half + 1):
            mine_here = summed[k, pl.ds(x, 1), PART:][0].astype(jnp.float32)
            for dx in (1, 3, 2):
                mine_here = mine_here + x_land[dx, k].astype(jnp.float32)
            z_terms[k] = mine_here.astype(jnp.bfloat16)
            if k < 3:
                z_copy2(k).start()

    arrived(2, rows_of(2, 0, 0, 32, columns(0, X_EARLY)))
    if Y_EARLY:
        send_parts(4, 0, 1, 0, Y_EARLY, rows_of(2, 0, 0, 32, columns(0, Y_EARLY)))
        send_parts(5, 0, 3, 0, Y_EARLY, rows_of(2, 0, 0, 32, columns(0, Y_EARLY)))

    first = x_terms[pl.ds(x, 1)][0].astype(jnp.float32)
    for dx in (1, 3, 2):
        x_copy2(dx).wait_recv()
        first = first + x_last[dx].astype(jnp.float32)
    rest = z_terms[3].astype(jnp.float32)
    for k in (1, 2, 0):
        z_copy2(k).wait_recv()
        rest = rest + z_last[k].astype(jnp.float32)
    y_terms[pl.ds(y, 1), :PART] = first.astype(jnp.bfloat16)[None]
    y_terms[pl.ds(y, 1), PART:] = rest.astype(jnp.bfloat16)[None]

    def y_copy(dy):
        return remote(y_terms.at[y], y_terms.at[y], y_send.at[dy], y_recv.at[dy], at(0, dy, 0))

    def send_opposite():
        arrived(6, rows_of(0, 2, 0, 16))
        arrived(7, rows_of(0, 2, 16, 16))
        if ACROSS:
            gather(10, 2, 0, rows_of(0, 2, 0, 32, columns(0, ACROSS)))
        to_sibling(4, shard(0, 2))

    for dy in (2, 1, 3):
        y_copy(dy).start()

    send_parts(3, 2, 0, X_EARLY, MIDDLE)
    send_parts(13, 2, 0, MIDDLE, width)
    arrived(0, shard(0, 3))
    gather(6, 0, 1, rows_of(0, 3, 0, 16))
    arrived(1, shard(0, 1))
    gather(7, 0, 3, rows_of(0, 1, 16, 16))
    to_sibling(1, shard(0, 3))
    to_sibling(2, shard(0, 1))
    for dy in (1, 3, 2):
        y_copy(dy).wait_recv()

    arrived(3, rows_of(2, 0, 0, 32, columns(X_EARLY, MIDDLE)))
    send_parts(8, 0, 1, Y_EARLY, MIDDLE, rows_of(2, 0, 0, 32, columns(Y_EARLY, MIDDLE)))
    send_parts(9, 0, 3, Y_EARLY, MIDDLE, rows_of(2, 0, 0, 32, columns(Y_EARLY, MIDDLE)))

    terms = [y_terms[i].astype(jnp.float32) for i in range(SIDE)]
    whole = (terms[0] + terms[1]) + (terms[2] + terms[3])
    c00, c01, c10, c11 = unpack(whole[:HALF], whole[HALF:BS], whole[BS : BS + 1])
    factor = jnp.concatenate(
        [jnp.concatenate([c00, c01], axis=1), jnp.concatenate([c10, c11], axis=1)], axis=0
    )
    block = core * CLASS + z * 4 + x
    counts.wait()
    mixed, off, diagonal = pack(newton(factor, count[block]))
    inv_own[:HALF] = mixed.astype(jnp.bfloat16)
    inv_own[HALF:BS] = off.astype(jnp.bfloat16)
    inv_own[BS:PACK] = diagonal.astype(jnp.bfloat16)
    inv_own[PACK:] = jnp.zeros((PACK_INV - PACK, HALF), jnp.bfloat16)

    upper, lower = pl.ds(0, PART), pl.ds(PART, PART)

    def agx_copy(d):
        return remote(inv_own.at[upper], inv_ref.at[core, z, x, upper], agx_send.at[d], agx_recv.at[d], at(d, 0, 0))

    def agz_copy(d):
        return remote(inv_own.at[lower], inv_ref.at[core, z, x, lower], agz_send.at[d], agz_recv.at[d], at(0, 0, d))

    def along_x(d):
        return inv_ref.at[core, (z + SIDE - d) % SIDE, :, upper]

    def along_z(d):
        return inv_ref.at[core, :, (x + SIDE - d) % SIDE, lower]

    def agz_copy2(d):
        return remote(along_x(0), along_x(0), agz2_send.at[d], agz2_recv.at[d], at(0, 0, d))

    def agx_copy2(d):
        return remote(along_z(0), along_z(0), agx2_send.at[d], agx2_recv.at[d], at(d, 0, 0))

    def pass_on(place, slot):
        return remote(place, place, ags_send.at[slot], ags_recv.at[slot], sibling)

    for d in (2, 1, 3):
        agx_copy(d).start()
        agz_copy(d).start()
    keep = pltpu.make_async_copy(inv_own, inv_ref.at[core, z, x], local_sem.at[1])
    keep.start()

    arrived(13, rows_of(2, 0, 0, 32, columns(MIDDLE, width)))
    send_parts(14, 0, 1, MIDDLE, width, rows_of(2, 0, 0, 32, columns(MIDDLE, width)))
    send_parts(15, 0, 3, MIDDLE, width, rows_of(2, 0, 0, 32, columns(MIDDLE, width)))
    to_sibling(3, shard(2, 0))
    keep.wait()
    for d in (1, 3, 2):
        agx_copy(d).wait_recv()
    for d in (2, 1, 3):
        agz_copy2(d).start()
    for d in (1, 3, 2):
        agz_copy(d).wait_recv()
    for d in (2, 1, 3):
        agx_copy2(d).start()
    pass_on(along_x(0), 0).start()
    pass_on(along_z(0), 4).start()
    send_opposite()
    for dy, one, two, three in ((3, 4, 8, 14), (1, 5, 9, 15)):
        if Y_EARLY:
            arrived(one, rows_of(2, dy, 0, 32, columns(0, Y_EARLY)))
        arrived(two, rows_of(2, dy, 0, 32, columns(Y_EARLY, MIDDLE)))
        arrived(three, rows_of(2, dy, 0, 32, columns(MIDDLE, width)))
        if ACROSS < width:
            first_row = 0 if dy == 3 else 16
            gather(11 + first_row // 16, 0, 4 - dy, rows_of(2, dy, first_row, 16, columns(ACROSS, width)))
        to_sibling(5 + first_row // 16 if ACROSS < width else 5 + dy // 2, shard(2, dy))
    for d in (1, 3, 2):
        agz_copy2(d).wait_recv()
        pass_on(along_x(d), d).start()
        agx_copy2(d).wait_recv()
        pass_on(along_z(d), 4 + d).start()
    if ACROSS:
        arrived(10, rows_of(2, 2, 0, 32, columns(0, ACROSS)))
    if ACROSS < width:
        arrived(11, rows_of(2, 2, 0, 16, columns(ACROSS, width)))
        arrived(12, rows_of(2, 2, 16, 16, columns(ACROSS, width)))
    to_sibling(7, shard(2, 2))

    mine.wait()
    for copy in gathers:
        copy.wait_send()
    for k in range(4):
        sib_copy(k).wait_send()
    for k in range(3):
        z_copy(k).wait_send()
        z_copy2(k).wait_send()
    for d in (1, 2, 3):
        x_copy(d, 0).wait_send()
        x_copy(d, 2).wait_send()
        x_copy2(d).wait_send()
        y_copy(d).wait_send()
        agx_copy(d).wait_send()
        agz_copy(d).wait_send()
        agx_copy2(d).wait_send()
        agz_copy2(d).wait_send()
    for d in range(4):
        pass_on(along_x(d), d).wait()
        pass_on(along_z(d), 4 + d).wait()
    for copy in passes:
        copy.wait()


def apply_kernel(inv_ref, grad_ref, out_ref, stage, sem):
    def block_copy(b):
        rows = pl.ds(b * BS, BS)
        return pltpu.make_async_copy(stage.at[rows], out_ref.at[rows], sem.at[b])

    for b in range(BLOCKS):
        packed = inv_ref[b].astype(jnp.float32)
        parts = unpack(packed[:HALF], packed[HALF:BS], packed[BS : BS + 1])
        c00, c01, c10, c11 = [part.astype(jnp.bfloat16) for part in parts]
        inverse = jnp.concatenate(
            [jnp.concatenate([c00, c01], axis=1), jnp.concatenate([c10, c11], axis=1)], axis=0
        )
        rows = grad_ref[:, b * BS : (b + 1) * BS]
        stage[b * BS : (b + 1) * BS] = lax.dot_general(
            inverse, rows, NT, preferred_element_type=jnp.float32
        ).astype(jnp.bfloat16)
        if b % WRITE == WRITE - 1:
            for w in range(b - WRITE + 1, b + 1):
                block_copy(w).start()
    for b in range(BLOCKS):
        block_copy(b).wait()


def per_device(activations, gradient, iterations):
    width = activations.shape[1]
    columns = gradient.shape[1] * 16
    anywhere = pl.BlockSpec(memory_space=pl.ANY)
    hbm = pl.BlockSpec(memory_space=pltpu.HBM)
    dma = pltpu.SemaphoreType.DMA
    full, inverses = pl.pallas_call(
        factor_kernel,
        name="factor",
        out_shape=[
            jax.ShapeDtypeStruct((columns, width), jnp.bfloat16),
            jax.ShapeDtypeStruct((2, SIDE, SIDE, PACK_INV, HALF), jnp.bfloat16),
        ],
        in_specs=[hbm, hbm, hbm],
        out_specs=[anywhere, anywhere],
        scratch_shapes=[
            pltpu.VMEM((8, activations.shape[0], GROUP_COLS), jnp.bfloat16),
            pltpu.VMEM((4, GROUP, PACK, HALF), jnp.bfloat16),
            pltpu.VMEM((4, GROUP, PACK, HALF), jnp.bfloat16),
            pltpu.VMEM((GROUP, PACK, HALF), jnp.float32),
            pltpu.VMEM((4, GROUP, PACK, HALF), jnp.bfloat16),
            pltpu.VMEM((3, GROUP, PART, HALF), jnp.bfloat16),
            pltpu.VMEM((SIDE, 4, PACK - PART, HALF), jnp.bfloat16),
            pltpu.VMEM((GROUP, PART, HALF), jnp.bfloat16),
            pltpu.VMEM((4, PACK - PART, HALF), jnp.bfloat16),
            pltpu.VMEM((SIDE, PART, HALF), jnp.bfloat16),
            pltpu.VMEM((3, PACK - PART, HALF), jnp.bfloat16),
            pltpu.VMEM((SIDE, PACK, HALF), jnp.bfloat16),
            pltpu.VMEM((PACK_INV, HALF), jnp.bfloat16),
            pltpu.SMEM((BLOCKS,), jnp.int32),
            dma((8,)), dma((4,)), dma((4,)), dma((3,)), dma((3,)), dma((4, 2)), dma((4, 2)), dma((4,)), dma((4,)),
            dma((4,)), dma((4,)), dma((3,)), dma((3,)),
            dma((4,)), dma((4,)), dma((4,)), dma((4,)), dma((4,)), dma((4,)), dma((4,)), dma((4,)), dma((8,)), dma((8,)),
            dma((3,)), dma((16,)), dma((16,)), dma((8,)), dma((8,)),
        ],
        compiler_params=pltpu.CompilerParams(
            collective_id=0, has_side_effects=True, vmem_limit_bytes=32 << 20
        ),
        cost_estimate=pl.CostEstimate(flops=5 * 10**9, bytes_accessed=32 << 20, transcendentals=0),
    )(activations, pltpu.with_memory_space_constraint(gradient.T, pltpu.HBM), pltpu.with_memory_space_constraint(iterations, pltpu.HBM))
    vmem = pl.BlockSpec(memory_space=pltpu.VMEM)
    return pl.pallas_call(
        apply_kernel,
        name="apply",
        out_shape=jax.ShapeDtypeStruct((width, columns), jnp.bfloat16),
        in_specs=[vmem, vmem],
        out_specs=pl.BlockSpec(memory_space=pltpu.HBM),
        scratch_shapes=[pltpu.VMEM((width, columns), jnp.bfloat16), dma((BLOCKS,))],
        compiler_params=pltpu.CompilerParams(vmem_limit_bytes=32 << 20),
        cost_estimate=pl.CostEstimate(flops=2 * 10**9, bytes_accessed=20 << 20, transcendentals=0),
    )(inverses.reshape(BLOCKS, PACK_INV, HALF), full)


def solution(mesh):
    placed = (P(("dp", "owner"), None), P(None, ("dp", "owner")), P())
    return jax.shard_map(
        per_device, mesh=mesh, in_specs=placed, out_specs=P(None, "dp"), check_vma=False
    )
```

```python
import functools

import jax
import jax.numpy as jnp
from jax import lax
from jax.experimental import pallas as pl
from jax.experimental.pallas import tpu as pltpu
from jax.sharding import PartitionSpec as P

BS = 256
HALF = BS // 2
BLOCKS = 32
PACK = BS + 16
PART = 144
PACK_INV = 2 * PART
TOKENS = 131072
DAMPING = 0.1
ITERS = 8
LEAST_ITERS = 5
SIDE = 4
GROUP = 4
GROUP_COLS = GROUP * BS
CLASS = 16
WRITE = 1
AHEAD = 4
AWAY = (2, 1, 3, 0)
X_EARLY = 2048
MIDDLE = 5120
Y_EARLY = 2048
ACROSS = 2048
MESH = pl.DeviceIdType.MESH

TN = (((0,), (0,)), ((), ()))
NT = (((1,), (1,)), ((), ()))


def here():
    shard = lax.axis_index("dp")
    owner = lax.axis_index("owner")
    x = (owner // 8) * 2 + shard % 2
    return x, (owner // 2) % 4, shard // 2, owner % 2


def mesh_id(x, y, z, core):
    return (z * 2 + x % 2, (x // 2) * 8 + y * 2 + core)


def owner_of(x, y, core):
    return (x // 2) * 8 + y * 2 + core


def tile_iota():
    rows = lax.broadcasted_iota(jnp.int32, (HALF, HALF), 0)
    cols = lax.broadcasted_iota(jnp.int32, (HALF, HALF), 1)
    return rows, cols


def pack(block):
    rows, cols = tile_iota()
    low = block[HALF:, HALF:]
    mixed = jnp.where(rows <= cols, block[:HALF, :HALF], low)
    diagonal = jnp.sum(jnp.where(rows == cols, low, 0.0), axis=0, keepdims=True)
    return mixed, block[:HALF, HALF:], jnp.broadcast_to(diagonal, (16, HALF))


def unpack(mixed, off, diagonal):
    rows, cols = tile_iota()
    turned = mixed.T
    first = jnp.where(rows <= cols, mixed, turned)
    second = jnp.where(rows > cols, mixed, jnp.where(rows < cols, turned, diagonal))
    return first, off, off.T, second


def split(value):
    high = value.astype(jnp.bfloat16)
    return high, (value - high.astype(jnp.float32)).astype(jnp.bfloat16)


def dot3(left, right):
    lh, ll = split(left)
    rh, rl = split(right)
    mul = functools.partial(jnp.dot, preferred_element_type=jnp.float32)
    return mul(lh, rh) + (mul(lh, rl) + mul(ll, rh))


def newton(factor, count):
    rows = lax.broadcasted_iota(jnp.int32, (BS, BS), 0)
    cols = lax.broadcasted_iota(jnp.int32, (BS, BS), 1)
    identity = jnp.where(rows == cols, 1.0, 0.0)
    damped = factor / TOKENS + DAMPING * identity
    bound = jnp.max(jnp.sum(jnp.abs(damped), axis=1))
    ratio = damped / bound
    approx = (2.0 * identity - ratio) / bound
    ratio = 2.0 * ratio - dot3(ratio, ratio)
    for step in range(1, ITERS):
        if step < ITERS - 1:
            both = dot3(jnp.concatenate([ratio, approx], axis=0), ratio)
            later = 2.0 * approx - both[BS:]
            ratio = 2.0 * ratio - both[:BS]
        else:
            later = 2.0 * approx - dot3(approx, ratio)
        approx = later if step < LEAST_ITERS else jnp.where(step < count, later, approx)
    return approx


def factor_kernel(
    act_ref, grad_ref, iters_ref,
    full_ref, inv_ref,
    act, to_sib, from_sib, own, summed, z_land, x_land, x_terms, z_terms, x_last, z_last, y_terms, inv_own, count,
    act_sem, sib_send, sib_recv, z_send, z_recv, x_send, x_recv, y_send, y_recv, x2_send, x2_recv, z2_send, z2_recv,
    agx_send, agx_recv, agz_send, agz_recv, agx2_send, agx2_recv, agz2_send, agz2_recv, ags_send, ags_recv,
    local_sem, g_send, g_recv, gs_send, gs_recv,
):
    x, y, z, core = here()
    sibling = mesh_id(x, y, z, 1 - core)

    def at(dx, dy, dz):
        return mesh_id((x + dx) % SIDE, (y + dy) % SIDE, (z + dz) % SIDE, core)

    def remote(src, dst, send, recv, target):
        return pltpu.make_async_remote_copy(
            src_ref=src, dst_ref=dst, send_sem=send, recv_sem=recv, device_id=target, device_id_type=MESH
        )

    work = [("sib", 0), ("sib", 1), ("own", 0), ("sib", 2), ("own", 1), ("sib", 3), ("own", 2), ("own", 3)]

    def act_copy(slot):
        kind, k = work[slot]
        side = 1 - core if kind == "sib" else core
        group = side * 4 + (z + AWAY[k]) % SIDE
        cols = pl.ds(pl.multiple_of(group * GROUP_COLS, GROUP_COLS), GROUP_COLS)
        return pltpu.make_async_copy(act_ref.at[:, cols], act.at[slot], act_sem.at[slot])

    for slot in range(AHEAD):
        act_copy(slot).start()
    counts = pltpu.make_async_copy(iters_ref, count, local_sem.at[2])
    counts.start()

    barrier = pltpu.get_barrier_semaphore()
    partners = [sibling]
    for d in (1, 2, 3):
        partners += [at(0, d, 0), at(d, 0, 0), at(0, 0, d)]
    for partner in partners:
        pl.semaphore_signal(barrier, inc=1, device_id=partner, device_id_type=MESH)

    def products(slot, store):
        act_copy(slot).wait()
        if slot + AHEAD < 8:
            act_copy(slot + AHEAD).start()
        for j in range(GROUP):
            cols = act[slot, :, j * BS : (j + 1) * BS]
            mixed, off, diagonal = pack(lax.dot_general(cols, cols, TN, preferred_element_type=jnp.float32))
            store(j, 0, HALF, mixed)
            store(j, HALF, HALF, off)
            store(j, BS, 16, diagonal)

    def sib_products(slot):
        k = work[slot][1]

        def store(j, first, rows, value):
            to_sib[k, j, first : first + rows] = value.astype(jnp.bfloat16)

        products(slot, store)

    sib_products(0)
    pl.semaphore_wait(barrier, len(partners))

    def rows_of(dx, dy, first, rows, cols=slice(None)):
        start = owner_of((x + dx) % SIDE, (y + dy) % SIDE, core) * 32 + first
        return full_ref.at[pl.ds(pl.multiple_of(start, 16), rows), cols]

    def shard(dx, dy):
        return rows_of(dx, dy, 0, 32)

    mine = pltpu.make_async_copy(grad_ref, shard(0, 0), local_sem.at[0])
    mine.start()
    gathers = []

    def gather(index, dx, dy, place, src=None):
        copy = remote(place if src is None else src, place, g_send.at[index], g_recv.at[index], at(dx, dy, 0))
        copy.start()
        gathers.append(copy)

    def arrived(index, place):
        remote(place, place, g_send.at[index], g_recv.at[index], at(0, 1, 0)).wait_recv()

    passes = []

    def to_sibling(index, place, src=None):
        copy = remote(place if src is None else src, place, gs_send.at[index], gs_recv.at[index], sibling)
        copy.start()
        passes.append(copy)

    def columns(first, last):
        return pl.ds(first, last - first)

    def send_parts(index, dx, dy, first, last, src=None):
        cols = columns(first, last)
        gather(index, dx, dy, rows_of(0, 0, 0, 32, cols) if src is None else src, grad_ref.at[:, cols] if src is None else None)

    width = grad_ref.shape[1]
    gather(0, 0, 1, shard(0, 0), grad_ref)
    gather(1, 0, 3, shard(0, 0), grad_ref)
    send_parts(2, 2, 0, 0, X_EARLY)

    def sib_copy(k):
        return remote(to_sib.at[k], from_sib.at[k], sib_send.at[k], sib_recv.at[k], sibling)

    def z_copy(k):
        return remote(summed.at[k, :, :PART], z_land.at[k], z_send.at[k], z_recv.at[k], at(0, 0, AWAY[k]))

    def x_copy(dx, k):
        return remote(
            summed.at[k : k + 2, (x + dx) % SIDE, PART:], x_land.at[dx, k : k + 2],
            x_send.at[dx, k // 2], x_recv.at[dx, k // 2], at(dx, 0, 0),
        )

    sib_copy(0).start()
    for slot in range(1, 8):
        kind, k = work[slot]
        if kind == "sib":
            sib_products(slot)
            sib_copy(k).start()
            continue

        def store_own(j, first, rows, value):
            own[j, first : first + rows] = value

        products(slot, store_own)
        sib_copy(k).wait_recv()
        summed[k] = (own[...] + from_sib[k].astype(jnp.float32)).astype(jnp.bfloat16)
        if k < 3:
            z_copy(k).start()
        if k % 2:
            for dx in (2, 1, 3):
                x_copy(dx, k - 1).start()

    to_sibling(0, shard(0, 0), grad_ref)

    totals = own[:, :PART] + from_sib[3, :, :PART].astype(jnp.float32)
    for k in range(3):
        z_copy(k).wait_recv()
        totals = totals + z_land[k].astype(jnp.float32)
    x_terms[...] = totals.astype(jnp.bfloat16)

    def x_copy2(dx):
        return remote(x_terms.at[(x + dx) % SIDE], x_last.at[dx], x2_send.at[dx], x2_recv.at[dx], at(dx, 0, 0))

    def z_copy2(k):
        return remote(z_terms.at[k], z_last.at[k], z2_send.at[k], z2_recv.at[k], at(0, 0, AWAY[k]))

    for dx in (2, 1, 3):
        x_copy2(dx).start()
    for half in (0, 2):
        for dx in (1, 3, 2):
            x_copy(dx, half).wait_recv()
        for k in (half, half + 1):
            mine_here = summed[k, pl.ds(x, 1), PART:][0].astype(jnp.float32)
            for dx in (1, 3, 2):
                mine_here = mine_here + x_land[dx, k].astype(jnp.float32)
            z_terms[k] = mine_here.astype(jnp.bfloat16)
            if k < 3:
                z_copy2(k).start()

    arrived(2, rows_of(2, 0, 0, 32, columns(0, X_EARLY)))
    if Y_EARLY:
        send_parts(4, 0, 1, 0, Y_EARLY, rows_of(2, 0, 0, 32, columns(0, Y_EARLY)))
        send_parts(5, 0, 3, 0, Y_EARLY, rows_of(2, 0, 0, 32, columns(0, Y_EARLY)))

    first = x_terms[pl.ds(x, 1)][0].astype(jnp.float32)
    for dx in (1, 3, 2):
        x_copy2(dx).wait_recv()
        first = first + x_last[dx].astype(jnp.float32)
    rest = z_terms[3].astype(jnp.float32)
    for k in (1, 2, 0):
        z_copy2(k).wait_recv()
        rest = rest + z_last[k].astype(jnp.float32)
    y_terms[pl.ds(y, 1), :PART] = first.astype(jnp.bfloat16)[None]
    y_terms[pl.ds(y, 1), PART:] = rest.astype(jnp.bfloat16)[None]

    def y_copy(dy):
        return remote(y_terms.at[y], y_terms.at[y], y_send.at[dy], y_recv.at[dy], at(0, dy, 0))

    def send_opposite():
        arrived(6, rows_of(0, 2, 0, 16))
        arrived(7, rows_of(0, 2, 16, 16))
        if ACROSS:
            gather(10, 2, 0, rows_of(0, 2, 0, 32, columns(0, ACROSS)))
        to_sibling(4, shard(0, 2))

    for dy in (2, 1, 3):
        y_copy(dy).start()

    send_parts(3, 2, 0, X_EARLY, MIDDLE)
    send_parts(13, 2, 0, MIDDLE, width)
    arrived(0, shard(0, 3))
    gather(6, 0, 1, rows_of(0, 3, 0, 16))
    arrived(1, shard(0, 1))
    gather(7, 0, 3, rows_of(0, 1, 16, 16))
    to_sibling(1, shard(0, 3))
    to_sibling(2, shard(0, 1))
    for dy in (1, 3, 2):
        y_copy(dy).wait_recv()

    arrived(3, rows_of(2, 0, 0, 32, columns(X_EARLY, MIDDLE)))
    send_parts(8, 0, 1, Y_EARLY, MIDDLE, rows_of(2, 0, 0, 32, columns(Y_EARLY, MIDDLE)))
    send_parts(9, 0, 3, Y_EARLY, MIDDLE, rows_of(2, 0, 0, 32, columns(Y_EARLY, MIDDLE)))

    terms = [y_terms[i].astype(jnp.float32) for i in range(SIDE)]
    whole = (terms[0] + terms[1]) + (terms[2] + terms[3])
    c00, c01, c10, c11 = unpack(whole[:HALF], whole[HALF:BS], whole[BS : BS + 1])
    factor = jnp.concatenate(
        [jnp.concatenate([c00, c01], axis=1), jnp.concatenate([c10, c11], axis=1)], axis=0
    )
    block = core * CLASS + z * 4 + x
    counts.wait()
    mixed, off, diagonal = pack(newton(factor, count[block]))
    inv_own[:HALF] = mixed.astype(jnp.bfloat16)
    inv_own[HALF:BS] = off.astype(jnp.bfloat16)
    inv_own[BS:PACK] = diagonal.astype(jnp.bfloat16)
    inv_own[PACK:] = jnp.zeros((PACK_INV - PACK, HALF), jnp.bfloat16)

    upper, lower = pl.ds(0, PART), pl.ds(PART, PART)

    def agx_copy(d):
        return remote(inv_own.at[upper], inv_ref.at[core, z, x, upper], agx_send.at[d], agx_recv.at[d], at(d, 0, 0))

    def agz_copy(d):
        return remote(inv_own.at[lower], inv_ref.at[core, z, x, lower], agz_send.at[d], agz_recv.at[d], at(0, 0, d))

    def along_x(d):
        return inv_ref.at[core, (z + SIDE - d) % SIDE, :, upper]

    def along_z(d):
        return inv_ref.at[core, :, (x + SIDE - d) % SIDE, lower]

    def agz_copy2(d):
        return remote(along_x(0), along_x(0), agz2_send.at[d], agz2_recv.at[d], at(0, 0, d))

    def agx_copy2(d):
        return remote(along_z(0), along_z(0), agx2_send.at[d], agx2_recv.at[d], at(d, 0, 0))

    def pass_on(place, slot):
        return remote(place, place, ags_send.at[slot], ags_recv.at[slot], sibling)

    for d in (2, 1, 3):
        agx_copy(d).start()
        agz_copy(d).start()
    keep = pltpu.make_async_copy(inv_own, inv_ref.at[core, z, x], local_sem.at[1])
    keep.start()

    arrived(13, rows_of(2, 0, 0, 32, columns(MIDDLE, width)))
    send_parts(14, 0, 1, MIDDLE, width, rows_of(2, 0, 0, 32, columns(MIDDLE, width)))
    send_parts(15, 0, 3, MIDDLE, width, rows_of(2, 0, 0, 32, columns(MIDDLE, width)))
    to_sibling(3, shard(2, 0))
    keep.wait()
    for d in (1, 3, 2):
        agx_copy(d).wait_recv()
    for d in (2, 1, 3):
        agz_copy2(d).start()
    for d in (1, 3, 2):
        agz_copy(d).wait_recv()
    for d in (2, 1, 3):
        agx_copy2(d).start()
    pass_on(along_x(0), 0).start()
    pass_on(along_z(0), 4).start()
    send_opposite()
    for dy, one, two, three in ((3, 4, 8, 14), (1, 5, 9, 15)):
        if Y_EARLY:
            arrived(one, rows_of(2, dy, 0, 32, columns(0, Y_EARLY)))
        arrived(two, rows_of(2, dy, 0, 32, columns(Y_EARLY, MIDDLE)))
        arrived(three, rows_of(2, dy, 0, 32, columns(MIDDLE, width)))
        if ACROSS < width:
            first_row = 0 if dy == 3 else 16
            gather(11 + first_row // 16, 0, 4 - dy, rows_of(2, dy, first_row, 16, columns(ACROSS, width)))
        to_sibling(5 + first_row // 16 if ACROSS < width else 5 + dy // 2, shard(2, dy))
    for d in (1, 3, 2):
        agz_copy2(d).wait_recv()
        pass_on(along_x(d), d).start()
        agx_copy2(d).wait_recv()
        pass_on(along_z(d), 4 + d).start()
    if ACROSS:
        arrived(10, rows_of(2, 2, 0, 32, columns(0, ACROSS)))
    if ACROSS < width:
        arrived(11, rows_of(2, 2, 0, 16, columns(ACROSS, width)))
        arrived(12, rows_of(2, 2, 16, 16, columns(ACROSS, width)))
    to_sibling(7, shard(2, 2))

    mine.wait()
    for copy in gathers:
        copy.wait_send()
    for k in range(4):
        sib_copy(k).wait_send()
    for k in range(3):
        z_copy(k).wait_send()
        z_copy2(k).wait_send()
    for d in (1, 2, 3):
        x_copy(d, 0).wait_send()
        x_copy(d, 2).wait_send()
        x_copy2(d).wait_send()
        y_copy(d).wait_send()
        agx_copy(d).wait_send()
        agz_copy(d).wait_send()
        agx_copy2(d).wait_send()
        agz_copy2(d).wait_send()
    for d in range(4):
        pass_on(along_x(d), d).wait()
        pass_on(along_z(d), 4 + d).wait()
    for copy in passes:
        copy.wait()


def apply_kernel(inv_ref, grad_ref, out_ref, stage, sem):
    def block_copy(b):
        rows = pl.ds(b * BS, BS)
        return pltpu.make_async_copy(stage.at[rows], out_ref.at[rows], sem.at[b])

    for b in range(BLOCKS):
        packed = inv_ref[b].astype(jnp.float32)
        parts = unpack(packed[:HALF], packed[HALF:BS], packed[BS : BS + 1])
        c00, c01, c10, c11 = [part.astype(jnp.bfloat16) for part in parts]
        inverse = jnp.concatenate(
            [jnp.concatenate([c00, c01], axis=1), jnp.concatenate([c10, c11], axis=1)], axis=0
        )
        rows = grad_ref[:, b * BS : (b + 1) * BS]
        stage[b * BS : (b + 1) * BS] = lax.dot_general(
            inverse, rows, NT, preferred_element_type=jnp.float32
        ).astype(jnp.bfloat16)
        if b % WRITE == WRITE - 1:
            for w in range(b - WRITE + 1, b + 1):
                block_copy(w).start()
    for b in range(BLOCKS):
        block_copy(b).wait()


def per_device(activations, gradient, iterations):
    width = activations.shape[1]
    columns = gradient.shape[1] * 16
    anywhere = pl.BlockSpec(memory_space=pl.ANY)
    hbm = pl.BlockSpec(memory_space=pltpu.HBM)
    dma = pltpu.SemaphoreType.DMA
    full, inverses = pl.pallas_call(
        factor_kernel,
        name="factor",
        out_shape=[
            jax.ShapeDtypeStruct((columns, width), jnp.bfloat16),
            jax.ShapeDtypeStruct((2, SIDE, SIDE, PACK_INV, HALF), jnp.bfloat16),
        ],
        in_specs=[hbm, hbm, hbm],
        out_specs=[anywhere, anywhere],
        scratch_shapes=[
            pltpu.VMEM((8, activations.shape[0], GROUP_COLS), jnp.bfloat16),
            pltpu.VMEM((4, GROUP, PACK, HALF), jnp.bfloat16),
            pltpu.VMEM((4, GROUP, PACK, HALF), jnp.bfloat16),
            pltpu.VMEM((GROUP, PACK, HALF), jnp.float32),
            pltpu.VMEM((4, GROUP, PACK, HALF), jnp.bfloat16),
            pltpu.VMEM((3, GROUP, PART, HALF), jnp.bfloat16),
            pltpu.VMEM((SIDE, 4, PACK - PART, HALF), jnp.bfloat16),
            pltpu.VMEM((GROUP, PART, HALF), jnp.bfloat16),
            pltpu.VMEM((4, PACK - PART, HALF), jnp.bfloat16),
            pltpu.VMEM((SIDE, PART, HALF), jnp.bfloat16),
            pltpu.VMEM((3, PACK - PART, HALF), jnp.bfloat16),
            pltpu.VMEM((SIDE, PACK, HALF), jnp.bfloat16),
            pltpu.VMEM((PACK_INV, HALF), jnp.bfloat16),
            pltpu.SMEM((BLOCKS,), jnp.int32),
            dma((8,)), dma((4,)), dma((4,)), dma((3,)), dma((3,)), dma((4, 2)), dma((4, 2)), dma((4,)), dma((4,)),
            dma((4,)), dma((4,)), dma((3,)), dma((3,)),
            dma((4,)), dma((4,)), dma((4,)), dma((4,)), dma((4,)), dma((4,)), dma((4,)), dma((4,)), dma((8,)), dma((8,)),
            dma((3,)), dma((16,)), dma((16,)), dma((8,)), dma((8,)),
        ],
        compiler_params=pltpu.CompilerParams(
            collective_id=0, has_side_effects=True, vmem_limit_bytes=32 << 20
        ),
        cost_estimate=pl.CostEstimate(flops=5 * 10**9, bytes_accessed=32 << 20, transcendentals=0),
    )(activations, pltpu.with_memory_space_constraint(gradient.T, pltpu.HBM), pltpu.with_memory_space_constraint(iterations, pltpu.HBM))
    vmem = pl.BlockSpec(memory_space=pltpu.VMEM)
    return pl.pallas_call(
        apply_kernel,
        name="apply",
        out_shape=jax.ShapeDtypeStruct((width, columns), jnp.bfloat16),
        in_specs=[vmem, vmem],
        out_specs=pl.BlockSpec(memory_space=pltpu.HBM),
        scratch_shapes=[pltpu.VMEM((width, columns), jnp.bfloat16), dma((BLOCKS,))],
        compiler_params=pltpu.CompilerParams(vmem_limit_bytes=32 << 20),
        cost_estimate=pl.CostEstimate(flops=2 * 10**9, bytes_accessed=20 << 20, transcendentals=0),
    )(inverses.reshape(BLOCKS, PACK_INV, HALF), full)


def solution(mesh):
    placed = (P(("dp", "owner"), None), P(None, ("dp", "owner")), P())
    return jax.shard_map(
        per_device, mesh=mesh, in_specs=placed, out_specs=P(None, "dp"), check_vma=False
    )
```
